128 devices in a mesh: gx: 32 (over z, y, core), gy: 4 (over x).
Axes of the slice: x: 4, y: 4, z: 4, core: 2. Of those that a mesh axis runs over, the one named last changes fastest.
Arguments:
- snapshot: float32 [512, 256, 512], P('gx', 'gy'), may hold values from -6 to 6
- keep_mask: int32 [512, 256, 4], P('gx', 'gy'), may hold values from 0 to 1, as said below
- exponents: int32 [4], replicated, may hold values from -1 to 2
Outputs:
- coefficients: float32 [512, 256, 512], P('gx', 'gy')
- stream: float32 [524288, 128], P(('gx', 'gy'))
The draws below stay inside these ranges and needn't reach their ends.
Inputs may be any that keep to these rules, and one draw needn't show every extreme that they name: `keep_mask`: each device block has its own keep rate.
All inputs are finite; a program needn't handle non-finite values.
Results may differ from the reference program's by a relative error of at most 0.0003.
Values sent between devices are 32-bit elements; how exact they have to be, the bound alone decides.
No kernel may reach another device: no remote copies, remote signals or barrier semaphores. Data moves between devices by JAX's collectives and lax.ppermute only.
A program may use at most 64 MiB of HBM per device.

```python
import jax
import jax.numpy as jnp
from jax import lax

X_DEV = 16
Y_DEV = 64
Z = 512
LEVELS = 3
TILE = 128
ZT = 4
NX = 512
NY = 256
SLOTS = 524288
N_GX = 32
N_GY = 4


def draw_keep_mask(key, part):
    key = jax.random.fold_in(key, 7)
    rate_key, flag_key = jax.random.split(key)
    keep_rate = jax.random.randint(rate_key, (NX // X_DEV, NY // Y_DEV), 3, 16)
    cell_rate = jnp.repeat(jnp.repeat(keep_rate, X_DEV, axis=0), Y_DEV, axis=1)
    uniform_bins = jax.random.randint(flag_key, (NX, NY, ZT), 0, 16)
    return (uniform_bins < cell_rate[:, :, None]).astype(jnp.int32)


def place_ends(array, stream_key, least, high):
    shape = array.shape
    index_at = [jax.random.randint(jax.random.fold_in(stream_key, axis), (), 0, shape[axis]) for axis in range(len(shape))]
    array = array.at[tuple(index_at)].set(least)
    longest = shape.index(max(shape))
    index_at[longest] = (index_at[longest] + 1) % shape[longest]
    return array.at[tuple(index_at)].set(high)


def level_of(key, extent, shards, least, top_value):
    loudness, own = 1.0, jax.random.fold_in(key, 6)
    for position, shards_of in shards:
        draws = jnp.exp(jax.random.uniform(jax.random.fold_in(own, position), (shards_of,), jnp.float32, least / len(shards), top_value / len(shards)))
        loudness = loudness * jnp.repeat(draws, extent[position] // shards_of).reshape([-1 if axis == position else 1 for axis in range(len(extent))])
    return loudness


def gaussian(rng, shape, width, reach, cuts=(), kind=jnp.bfloat16):
    factor_of = level_of(rng, shape, cuts, -0.22, 0.18) if cuts else 1.0
    drawn = jax.random.normal(rng, shape, jnp.float32) * width * factor_of
    return jnp.minimum(jnp.maximum(drawn, -reach), reach).astype(kind)


def setup_inputs(seed: int = 0) -> dict:
    streams_of = jax.random.split(jax.random.key(seed), 4)
    return {
        "snapshot": gaussian(streams_of[0], (NX, NY, Z), 1.0, 6.0, ((0, 32), (1, 4)), jnp.float32),
        "keep_mask": draw_keep_mask(jax.random.fold_in(streams_of[3], 71), 0),
        "exponents": place_ends(jax.random.randint(streams_of[2], (LEVELS + 1,), -1, 3), jax.random.fold_in(streams_of[2], 1), -1, 2).astype(jnp.int32),
    }


def split_pair(values, dim):
    dims_now = values.shape
    paired = values.reshape(dims_now[:dim] + (dims_now[dim] // 2, 2) + dims_now[dim + 1:])
    return lax.index_in_dim(paired, 0, dim + 1, keepdims=False), lax.index_in_dim(paired, 1, dim + 1, keepdims=False)


def alternate(first, second, dim):
    stacked = jnp.stack([first, second], axis=dim + 1)
    dims_now = first.shape
    return stacked.reshape(dims_now[:dim] + (dims_now[dim] * 2,) + dims_now[dim + 1:])


def lift_dim(values, dim):
    even_part, odd_part = split_pair(values, dim)
    length = even_part.shape[dim]
    zero_row = jnp.zeros_like(lax.slice_in_dim(even_part, 0, 1, axis=dim))
    ahead = jnp.concatenate([lax.slice_in_dim(even_part, 1, length, axis=dim), zero_row], axis=dim)
    detail = odd_part - 0.5 * (even_part + ahead)
    behind = jnp.concatenate([zero_row, lax.slice_in_dim(detail, 0, length - 1, axis=dim)], axis=dim)
    smooth = even_part + 0.25 * (behind + detail)
    return smooth, detail


def decompose(values, depth):
    smooth_x, detail_x = lift_dim(values, 0)
    smooth_xy, detail_y = lift_dim(smooth_x, 1)
    coarse = decompose(smooth_xy, depth + 1) if depth + 1 < LEVELS else smooth_xy
    merged = alternate(coarse, detail_y, 1)
    return alternate(merged, detail_x, 0)


def reference(snapshot, keep_mask, exponents):
    layout = decompose(snapshot, 0)
    x_index = jnp.arange(NX, dtype=jnp.int32)
    y_index = jnp.arange(NY, dtype=jnp.int32)
    joined = jnp.bitwise_or(x_index[:, None], y_index[None, :])
    level_code = (joined % 2 == 0).astype(jnp.int32) + (joined % 4 == 0).astype(jnp.int32) + (joined % 8 == 0).astype(jnp.int32)
    factor = jnp.zeros((NX, NY), jnp.float32)
    for level_no in range(LEVELS + 1):
        factor = factor + jnp.where(level_code == level_no, jnp.exp2(exponents[level_no].astype(jnp.float32)), jnp.float32(0.0))
    coefficients = layout * factor[:, :, None]
    ordered = coefficients.reshape(N_GX, X_DEV, N_GY, Y_DEV, ZT, TILE).transpose(0, 2, 1, 3, 4, 5).reshape(SLOTS, TILE)
    flags = keep_mask.reshape(N_GX, X_DEV, N_GY, Y_DEV, ZT).transpose(0, 2, 1, 3, 4).reshape(SLOTS)
    ranks = (jnp.cumsum(flags) - flags).astype(jnp.int32)
    target = jnp.where(flags > 0, ranks, jnp.int32(SLOTS)).astype(jnp.int32)
    stream = jnp.zeros((SLOTS, TILE), jnp.float32).at[target].add(ordered, mode="drop")
    return coefficients, stream
```

```python
import jax
import jax.numpy as jnp
from jax import lax
from jax.experimental import pallas as pl
from jax.experimental.pallas import tpu as pltpu
from jax.sharding import PartitionSpec as P

ALL = ("gx", "gy")
SUB = 8
LANES = 128
VMEM = pl.BlockSpec(memory_space=pltpu.VMEM)
SMEM = pl.BlockSpec(memory_space=pltpu.SMEM)
PARAMS = pltpu.CompilerParams(vmem_limit_bytes=48 * 2**20)


def shifted(value, axis, steps):
    count = lax.axis_size(axis)
    leading, last = (max(0, -steps), min(count, count - steps))
    return lax.ppermute(value, axis, [(source, source + steps) for source in range(leading, last)])


def sublane():
    return lax.broadcasted_iota(jnp.int32, (SUB, LANES), 0)


def rolled(tile, steps):
    return pltpu.roll(tile, steps % SUB, 0)


def neighbours(tiles, s, sub):
    up = [rolled(t, -s) for t in tiles]
    down = up if 2 * s == SUB else [rolled(t, s) for t in tiles]
    return [
        jnp.where(sub < SUB - s, up[k], up[k + 1]) + jnp.where(sub >= s, down[k], down[k - 1])
        for k in range(1, len(tiles) - 1)
    ]


def weight(value, chosen):
    return jnp.where(chosen, jnp.float32(value), jnp.float32(0.0))


def lift_rows(tiles, s, sub, has_left, has_right):
    odd = weight(0.5, sub % (2 * s) == s)
    even = weight(0.25, sub % (2 * s) == 0)
    left, right = tiles[0], tiles[-1]
    inner = [t - odd * n for t, n in zip(tiles[1:-1], neighbours(tiles, s, sub))]
    ahead = rolled(tiles[1], -s)
    left = left - jnp.where(sub == SUB - s, 0.5 * has_left * ahead, 0.0)
    full = [left] + inner + [right]
    smooth = [t + even * n for t, n in zip(inner, neighbours(full, s, sub))]
    behind = rolled(inner[-1], s)
    if s == 1:
        right = jnp.where(sub == 0, rolled(right, -1) + 0.25 * has_right * behind, right)
        left = left + jnp.where(sub == SUB - 2, 0.25 * rolled(left, -1), 0.0)
    elif s == 2:
        right = jnp.where(
            sub == 0, 0.875 * right + rolled(right, -2) + 0.25 * has_right * behind, right
        )
        left = left + jnp.where(sub == SUB - 4, 0.25 * rolled(left, -2), 0.0)
    return [left] + smooth + [right]


def combine(first, second, scale):
    return [a + scale * b for a, b in zip(first, second)]


def front_parts(c):
    d1, d3, d5 = (combine(c[k], combine(c[k - 1], c[k + 1], 1.0), -0.5) for k in (1, 3, 5))
    c2 = combine(c[2], combine(d1, d3, 1.0), 0.25)
    c4 = combine(c[4], combine(d3, d5, 1.0), 0.25)
    third = [0.25 * (a - 0.5 * b) for a, b in zip(c2, c4)]
    return c[0], combine(c[0], d1, 0.25), third


def back_parts(c):
    d = {k: combine(c[k], combine(c[k - 1], c[k + 1], 1.0), -0.5) for k in (3, 5, 7, 9, 11, 13)}
    e = {k: combine(c[k], combine(d[k - 1], d[k + 1], 1.0), 0.25) for k in (4, 6, 8, 10, 12)}
    d6 = combine(e[6], combine(e[4], e[8], 1.0), -0.5)
    d10 = combine(e[10], combine(e[8], e[12], 1.0), -0.5)
    f8 = combine(e[8], combine(d6, d10, 1.0), 0.25)
    first = combine(c[15], c[14], -0.5)
    second = combine(combine(c[14], d[13], 0.25), e[12], -0.5)
    third = combine(combine(e[12], d10, 0.25), f8, -0.5)
    return first, second, third


def y_edges_kernel(head_ref, tail_ref, to_before_ref, to_after_ref):
    rows = head_ref.shape[0]
    half = rows // 2
    sub = sublane()
    zero = jnp.zeros((SUB, LANES), jnp.float32)

    def before(x, lanes):
        v = head_ref[x, :, lanes]
        d1 = v - weight(0.5, sub % 2 == 1) * (rolled(v, -1) + rolled(v, 1))
        c2 = d1 + 0.25 * (rolled(d1, -1) + rolled(d1, 1))
        second = rolled(v, 1) + 0.25 * d1
        third = 0.25 * (c2 - 0.5 * rolled(c2, -2))
        return jnp.where(
            sub == 0, v, jnp.where(sub == 1, second, jnp.where(sub == 2, third, 0.0))
        )

    def after(x, lanes):
        v = [zero, tail_ref[x, :SUB, lanes], tail_ref[x, SUB:, lanes], zero]
        odd = weight(0.5, sub % 2 == 1)
        d = [zero] + [t - odd * n for t, n in zip(v[1:-1], neighbours(v, 1, sub))] + [zero]
        even = weight(0.25, sub % 2 == 0)
        e = [zero] + [t + even * n for t, n in zip(d[1:-1], neighbours(d, 1, sub))] + [zero]
        odd = weight(0.5, sub % 4 == 2)
        f = [zero] + [t - odd * n for t, n in zip(e[1:-1], neighbours(e, 2, sub))] + [zero]
        even = weight(0.25, sub % 4 == 0)
        g = [t + even * n for t, n in zip(f[1:-1], neighbours(f, 2, sub))]
        first = d[2]
        second = v[2] + 0.25 * rolled(d[2], 1) - 0.5 * rolled(e[2], 2)
        third = e[2] + 0.25 * rolled(f[2], 2) - 0.5 * rolled(g[1], 4)
        return jnp.where(
            sub == 7, first, jnp.where(sub == 6, second, jnp.where(sub == 4, third, 0.0))
        )

    @pl.loop(0, half)
    def _(x):
        for t in range(head_ref.shape[2] // LANES):
            lanes = slice(t * LANES, (t + 1) * LANES)
            to_before_ref[x, :, lanes] = before(x, lanes) + rolled(before(x + half, lanes), 4)
            to_after_ref[x, :, lanes] = after(x, lanes) + rolled(after(x + half, lanes), 4)


def y_edges(snapshot):
    rows, cols, depth = snapshot.shape
    shape = jax.ShapeDtypeStruct((rows // 2, SUB, depth), jnp.float32)
    return pl.pallas_call(
        y_edges_kernel,
        grid=(1,),
        in_specs=[
            pl.BlockSpec((rows, SUB, depth), lambda i: (0, 0, 0)),
            pl.BlockSpec((rows, 2 * SUB, depth), lambda i: (0, cols // (2 * SUB) - 1, 0)),
        ],
        out_specs=[pl.BlockSpec(shape.shape, lambda i: (0, 0, 0))] * 2,
        out_shape=[shape] * 2,
        compiler_params=PARAMS,
        name="y_edges",
    )(snapshot, snapshot)


def row_of(snapshot_ref, left_ref, right_ref, x, lanes, sub):
    rows, cols, _ = snapshot_ref.shape
    half = rows // 2
    left = left_ref[x % half, :, lanes]
    right = right_ref[x % half, :, lanes]
    if x >= half:
        left, right = rolled(left, 4), rolled(right, 4)
    left = jnp.where(sub >= 4, left, 0.0)
    right = jnp.where(sub < 4, right, 0.0)
    inner = [snapshot_ref[x, SUB * k : SUB * (k + 1), lanes] for k in range(cols // SUB)]
    return [left] + inner + [right]


def x_edges_kernel(snapshot_ref, left_ref, right_ref, to_before_ref, to_after_ref):
    rows, cols, depth = snapshot_ref.shape
    sub = sublane()
    half = rows // 2
    count = cols // SUB

    def tile(x, k, lanes):
        if k == 0:
            left = left_ref[x % half, :, lanes]
            return jnp.where(sub >= 4, rolled(left, 4) if x >= half else left, 0.0)
        if k == count + 1:
            right = right_ref[x % half, :, lanes]
            return jnp.where(sub < 4, rolled(right, 4) if x >= half else right, 0.0)
        return snapshot_ref[x, SUB * (k - 1) : SUB * k, lanes]

    @pl.loop(0, depth // LANES)
    def _(t):
        lanes = pl.ds(pl.multiple_of(t * LANES, LANES), LANES)
        for k in range(count + 2):
            c = {x: [tile(x, k, lanes)] for x in range(rows)}
            for level, (a, b) in enumerate(zip(front_parts(c), back_parts(c))):
                to_before_ref[level, SUB * k : SUB * (k + 1), lanes] = a[0]
                to_after_ref[level, SUB * k : SUB * (k + 1), lanes] = b[0]


def x_edges(snapshot, left, right):
    rows, cols, depth = snapshot.shape
    shape = jax.ShapeDtypeStruct((3, cols + 2 * SUB, depth), jnp.float32)
    return pl.pallas_call(
        x_edges_kernel,
        in_specs=[VMEM] * 3,
        out_specs=[VMEM] * 2,
        out_shape=[shape] * 2,
        compiler_params=PARAMS,
        name="x_edges",
    )(snapshot, left, right)


def main_kernel(
    counts_ref,
    row_counts_ref,
    scales_ref,
    snapshot_ref,
    left_ref,
    right_ref,
    before_ref,
    after_ref,
    flags_ref,
    coefficients_ref,
    packed_ref,
    buffer,
    ranks,
):
    rows, cols, depth = snapshot_ref.shape
    slots = packed_ref.shape[0]
    width = depth // LANES
    count = cols // SUB
    per_row = cols * width
    sub = sublane()
    gx, gy = lax.axis_index("gx"), lax.axis_index("gy")
    one, zero = jnp.float32(1.0), jnp.float32(0.0)
    x_left = jnp.where(gx > 0, one, zero)
    x_right = jnp.where(gx < lax.axis_size("gx") - 1, one, zero)
    y_left = jnp.where(gy > 0, one, zero)
    y_right = jnp.where(gy < lax.axis_size("gy") - 1, one, zero)
    device = gx * lax.axis_size("gy") + gy

    scale = [scales_ref[k] for k in range(4)]
    factor = {8: jnp.where(sub % 8 == 0, scale[3], scale[2])}
    factor[4] = jnp.where(sub % 4 == 0, scale[2], scale[1])
    factor[2] = jnp.where(sub % 2 == 0, scale[1], scale[0])
    factor[8] = jnp.where(sub % 4 == 0, factor[8], factor[2])
    factor[4] = jnp.where(sub % 4 == 0, factor[4], factor[2])
    factor[1] = jnp.where(sub % 2 == 0, scale[0], scale[0])
    factor[8] = jnp.where(sub % 2 == 0, factor[8], scale[0])
    factor[4] = jnp.where(sub % 2 == 0, factor[4], scale[0])

    @pl.loop(0, width)
    def _(t):
        lanes = pl.ds(pl.multiple_of(t * LANES, LANES), LANES)

        def load(ref, level):
            return [ref[level, SUB * k : SUB * (k + 1), lanes] for k in range(count + 2)]

        def store(x, row):
            by = 8 if x % 8 == 0 else 4 if x % 4 == 0 else 2 if x % 2 == 0 else 1
            for k in range(count):
                coefficients_ref[x, SUB * k : SUB * (k + 1), lanes] = factor[by] * row[k + 1]

        def step(c, s, beyond, ahead, mine):
            held = sub % s == 0
            half_w, quarter_w = weight(0.5, held), weight(0.25, held)
            end = rows
            c[end] = beyond
            for x in range(s, rows, 2 * s):
                c[x] = [v - half_w * (a + b) for v, a, b in zip(c[x], c[x - s], c[x + s])]
            c[-s] = [v - (half_w * x_left) * a for v, a in zip(ahead, c[0])]
            for x in range(0, rows, 2 * s):
                c[x] = [v + quarter_w * (a + b) for v, a, b in zip(c[x], c[x - s], c[x + s])]
            past = [v + (0.25 * x_right) * a for v, a in zip(mine, c[rows - s])] if mine else None
            return c, past, c[-s]

        def lift(row, s):
            return lift_rows(row, s, sub, y_left, y_right)

        c = {x: row_of(snapshot_ref, left_ref, right_ref, x, lanes, sub) for x in range(rows)}
        c, past, d = step(c, 1, load(after_ref, 0), load(before_ref, 0), load(after_ref, 1))
        for x in range(1, rows, 2):
            store(x, c[x])
        kept = combine(load(before_ref, 1), d, 0.25)
        for x in range(0, rows, 2):
            c[x] = lift(c[x], 1)
        past, kept = lift(past, 1), lift(kept, 1)
        after3, before3 = lift(load(after_ref, 2), 1), lift(load(before_ref, 2), 1)
        mine = [0.875 * v + a for v, a in zip(past, after3)]
        c, past, d = step(c, 2, past, kept, mine)
        for x in range(2, rows, 4):
            store(x, c[x])
        kept = combine(before3, d, 0.25)
        for x in range(0, rows, 4):
            c[x] = lift(c[x], 2)
        past, kept = lift(past, 2), lift(kept, 2)
        c, past, d = step(c, 4, past, kept, None)
        for x in range(4, rows, 8):
            store(x, c[x])
        for x in range(0, rows, 8):
            store(x, lift(c[x], 4))

    buffer[...] = jnp.zeros_like(buffer)
    flags = flags_ref[...]
    source = lax.broadcasted_iota(jnp.int32, (per_row, per_row), 0)
    target = lax.broadcasted_iota(jnp.int32, (per_row, per_row), 1)
    source = source % cols * width + source // cols
    target = target % cols * width + target // cols
    earlier = jnp.where(source < target, one, zero).astype(jnp.bfloat16)
    place = jnp.dot(flags.astype(jnp.bfloat16), earlier, preferred_element_type=jnp.float32)
    ranks[...] = jnp.where(flags > 0, place.astype(jnp.int32), -per_row)

    start = lax.fori_loop(0, device, lambda s, total: total + counts_ref[s], jnp.int32(0))
    span = per_row + SUB

    def pack(x, start):
        at = start % slots
        base = pl.multiple_of(at // SUB * SUB, SUB)
        wanted = ranks[pl.ds(x, 1), :] + (at - base)
        row_id = lax.broadcasted_iota(jnp.int32, (span, per_row), 0)
        onehot = jnp.where(row_id == wanted, one, zero).astype(jnp.bfloat16)
        values = jnp.concatenate(
            [coefficients_ref[x, :, LANES * t : LANES * (t + 1)] for t in range(width)], axis=0
        )
        high = values.astype(jnp.bfloat16)
        low = (values - high.astype(jnp.float32)).astype(jnp.bfloat16)
        both = jnp.dot(
            onehot, jnp.concatenate([high, low], axis=1), preferred_element_type=jnp.float32
        )
        buffer[pl.ds(base, span), :] += both[:, :LANES] + both[:, LANES:]
        return start + row_counts_ref[x]

    lax.fori_loop(0, rows, pack, start)
    packed_ref[span:, :] = buffer[span:slots, :]
    packed_ref[:span, :] = buffer[:span, :] + buffer[slots:, :]


def main(counts, row_counts, scales, snapshot, left, right, before, after, flags):
    rows, cols, depth = snapshot.shape
    per_row = flags.shape[1]
    slots = rows * per_row
    return pl.pallas_call(
        main_kernel,
        in_specs=[SMEM] * 3 + [VMEM] * 6,
        out_specs=[VMEM] * 2,
        out_shape=[
            jax.ShapeDtypeStruct(snapshot.shape, jnp.float32),
            jax.ShapeDtypeStruct((slots, LANES), jnp.float32),
        ],
        scratch_shapes=[
            pltpu.VMEM((slots + per_row + SUB, LANES), jnp.float32),
            pltpu.VMEM((rows, per_row), jnp.int32),
        ],
        compiler_params=PARAMS,
        name="lift_and_pack",
    )(counts, row_counts, scales, snapshot, left, right, before, after, flags)


def merge_kernel(counts_ref, arrived_ref, merged_ref, buffer):
    devices, share, _ = arrived_ref.shape
    slots = devices * share
    device = lax.axis_index("gx") * lax.axis_size("gy") + lax.axis_index("gy")
    buffer[...] = jnp.zeros_like(buffer)
    row_id = lax.broadcasted_iota(jnp.int32, (share, LANES), 0)

    def one(s, start):
        block = start // slots
        first = start % slots - device * share
        rows = arrived_ref[s]
        here = row_id >= first
        buffer[block] += jnp.where(here, rows, 0.0)
        buffer[block + 1] += jnp.where(here, 0.0, rows)
        return start + counts_ref[s]

    lax.fori_loop(0, devices, one, jnp.int32(0))
    merged_ref[...] = buffer[:devices]


def merge(counts, arrived):
    devices, share, _ = arrived.shape
    return pl.pallas_call(
        merge_kernel,
        in_specs=[SMEM, VMEM],
        out_specs=VMEM,
        out_shape=jax.ShapeDtypeStruct(arrived.shape, jnp.float32),
        scratch_shapes=[pltpu.VMEM((devices + 2, share, LANES), jnp.float32)],
        compiler_params=PARAMS,
        name="merge",
    )(counts, arrived)


def on_device(snapshot, keep_mask, exponents):
    rows, cols, depth = snapshot.shape
    width = keep_mask.shape[2]
    devices = lax.axis_size("gx") * lax.axis_size("gy")
    slots = rows * cols * width
    to_before, to_after = y_edges(snapshot)
    right = shifted(to_before, "gy", -1)
    left = shifted(to_after, "gy", 1)
    row_counts = jnp.sum(keep_mask, axis=(1, 2))
    own = jnp.sum(row_counts)
    counts = lax.all_to_all(jnp.full((devices,), own, jnp.int32), ALL, 0, 0, tiled=True)
    flags = keep_mask.transpose(0, 2, 1).reshape(rows, cols * width)
    scales = jnp.exp2(exponents.astype(jnp.float32))
    x_before, x_after = x_edges(snapshot, left, right)
    after = shifted(x_before, "gx", -1)
    before = shifted(x_after, "gx", 1)
    coefficients, packed = main(
        counts, row_counts, scales, snapshot, left, right, before, after, flags
    )
    share = slots // devices
    arrived = lax.all_to_all(packed.reshape(devices, share, LANES), ALL, 0, 0, tiled=True)
    merged = merge(counts, arrived)
    stream = lax.all_to_all(merged, ALL, 0, 0, tiled=True).reshape(slots, LANES)
    return coefficients, stream


def solution(mesh):
    in_specs = (P("gx", "gy", None), P("gx", "gy", None), P())
    out_specs = (P("gx", "gy", None), P(("gx", "gy"), None))
    return jax.shard_map(
        on_device, mesh=mesh, in_specs=in_specs, out_specs=out_specs, check_vma=False
    )
```

```python
import jax
import jax.numpy as jnp
from jax import lax
from jax.experimental import pallas as pl
from jax.experimental.pallas import tpu as pltpu
from jax.sharding import PartitionSpec as P

ALL = ("gx", "gy")
SUB = 8
LANES = 128
TURN = 64
VMEM = pl.BlockSpec(memory_space=pltpu.VMEM)
SMEM = pl.BlockSpec(memory_space=pltpu.SMEM)
PARAMS = pltpu.CompilerParams(vmem_limit_bytes=16 * 2**20)


def shifted(value, axis, steps):
    count = lax.axis_size(axis)
    leading, last = (max(0, -steps), min(count, count - steps))
    return lax.ppermute(value, axis, [(source, source + steps) for source in range(leading, last)])


def sublane():
    return lax.broadcasted_iota(jnp.int32, (SUB, LANES), 0)


def rolled(tile, steps):
    return pltpu.roll(tile, steps % SUB, 0)


def neighbours(tiles, s, sub):
    up = [rolled(t, -s) for t in tiles]
    down = up if 2 * s == SUB else [rolled(t, s) for t in tiles]
    return [
        jnp.where(sub < SUB - s, up[k], up[k + 1]) + jnp.where(sub >= s, down[k], down[k - 1])
        for k in range(1, len(tiles) - 1)
    ]


def weight(value, chosen):
    return jnp.where(chosen, jnp.float32(value), jnp.float32(0.0))


def lift_rows(tiles, s, sub, has_left, has_right):
    odd = weight(0.5, sub % (2 * s) == s)
    even = weight(0.25, sub % (2 * s) == 0)
    left, right = tiles[0], tiles[-1]
    inner = [t - odd * n for t, n in zip(tiles[1:-1], neighbours(tiles, s, sub))]
    ahead = rolled(tiles[1], -s)
    left = left - jnp.where(sub == SUB - s, 0.5 * has_left * ahead, 0.0)
    full = [left] + inner + [right]
    smooth = [t + even * n for t, n in zip(inner, neighbours(full, s, sub))]
    behind = rolled(inner[-1], s)
    if s == 1:
        right = jnp.where(sub == 0, rolled(right, -1) + 0.25 * has_right * behind, right)
        left = left + jnp.where(sub == SUB - 2, 0.25 * rolled(left, -1), 0.0)
    elif s == 2:
        right = jnp.where(
            sub == 0, 0.875 * right + rolled(right, -2) + 0.25 * has_right * behind, right
        )
        left = left + jnp.where(sub == SUB - 4, 0.25 * rolled(left, -2), 0.0)
    return [left] + smooth + [right]


def combine(first, second, scale):
    return [a + scale * b for a, b in zip(first, second)]


def front_parts(c):
    d1, d3, d5 = (combine(c[k], combine(c[k - 1], c[k + 1], 1.0), -0.5) for k in (1, 3, 5))
    c2 = combine(c[2], combine(d1, d3, 1.0), 0.25)
    c4 = combine(c[4], combine(d3, d5, 1.0), 0.25)
    third = [0.25 * (a - 0.5 * b) for a, b in zip(c2, c4)]
    return c[0], combine(c[0], d1, 0.25), third


def back_parts(c):
    d = {k: combine(c[k], combine(c[k - 1], c[k + 1], 1.0), -0.5) for k in (3, 5, 7, 9, 11, 13)}
    e = {k: combine(c[k], combine(d[k - 1], d[k + 1], 1.0), 0.25) for k in (4, 6, 8, 10, 12)}
    d6 = combine(e[6], combine(e[4], e[8], 1.0), -0.5)
    d10 = combine(e[10], combine(e[8], e[12], 1.0), -0.5)
    f8 = combine(e[8], combine(d6, d10, 1.0), 0.25)
    first = combine(c[15], c[14], -0.5)
    second = combine(combine(c[14], d[13], 0.25), e[12], -0.5)
    third = combine(combine(e[12], d10, 0.25), f8, -0.5)
    return first, second, third


def y_edges_kernel(
    snapshot_ref,
    mask_ref,
    to_before_ref,
    to_after_ref,
    counts_ref,
    starts_ref,
    head_ref,
    tail_ref,
    sems,
):
    rows, cols, depth = snapshot_ref.shape
    half = rows // 2
    copies = [
        pltpu.make_async_copy(snapshot_ref.at[:, :SUB, :], head_ref, sems.at[0]),
        pltpu.make_async_copy(snapshot_ref.at[:, cols - 2 * SUB :, :], tail_ref, sems.at[1]),
    ]
    for copy in copies:
        copy.start()
    sub = sublane()
    zero = jnp.zeros((SUB, LANES), jnp.float32)

    kept = mask_ref[:, 0, :]
    for t in range(1, mask_ref.shape[1]):
        kept = kept + mask_ref[:, t, :]
    kept = jnp.sum(kept.astype(jnp.float32), axis=1, keepdims=True)
    kept = jnp.broadcast_to(kept, (rows, LANES))
    shape = (rows, rows)
    later = lax.broadcasted_iota(jnp.int32, shape, 0) > lax.broadcasted_iota(jnp.int32, shape, 1)
    later = jnp.where(later, jnp.float32(1.0), jnp.float32(0.0)).astype(jnp.bfloat16)
    starts = jnp.dot(later, kept.astype(jnp.bfloat16), preferred_element_type=jnp.float32)
    starts_ref[...] = starts.astype(jnp.int32)
    total = (starts[rows - 1 :, :] + kept[rows - 1 :, :]).astype(jnp.int32)
    counts_ref[...] = jnp.broadcast_to(total, counts_ref.shape)

    def before(x, lanes):
        v = head_ref[x, :, lanes]
        d1 = v - weight(0.5, sub % 2 == 1) * (rolled(v, -1) + rolled(v, 1))
        c2 = d1 + 0.25 * (rolled(d1, -1) + rolled(d1, 1))
        second = rolled(v, 1) + 0.25 * d1
        third = 0.25 * (c2 - 0.5 * rolled(c2, -2))
        return jnp.where(
            sub == 0, v, jnp.where(sub == 1, second, jnp.where(sub == 2, third, 0.0))
        )

    def after(x, lanes):
        v = [zero, tail_ref[x, :SUB, lanes], tail_ref[x, SUB:, lanes], zero]
        odd = weight(0.5, sub % 2 == 1)
        d = [zero] + [t - odd * n for t, n in zip(v[1:-1], neighbours(v, 1, sub))] + [zero]
        even = weight(0.25, sub % 2 == 0)
        e = [zero] + [t + even * n for t, n in zip(d[1:-1], neighbours(d, 1, sub))] + [zero]
        odd = weight(0.5, sub % 4 == 2)
        f = [zero] + [t - odd * n for t, n in zip(e[1:-1], neighbours(e, 2, sub))] + [zero]
        even = weight(0.25, sub % 4 == 0)
        g = [t + even * n for t, n in zip(f[1:-1], neighbours(f, 2, sub))]
        first = d[2]
        second = v[2] + 0.25 * rolled(d[2], 1) - 0.5 * rolled(e[2], 2)
        third = e[2] + 0.25 * rolled(f[2], 2) - 0.5 * rolled(g[1], 4)
        return jnp.where(
            sub == 7, first, jnp.where(sub == 6, second, jnp.where(sub == 4, third, 0.0))
        )

    for copy in copies:
        copy.wait()

    @pl.loop(0, half)
    def _(x):
        for t in range(depth // LANES):
            lanes = slice(t * LANES, (t + 1) * LANES)
            to_before_ref[x, :, lanes] = before(x, lanes) + rolled(before(x + half, lanes), 4)
            to_after_ref[x, :, lanes] = after(x, lanes) + rolled(after(x + half, lanes), 4)


def y_edges(snapshot, mask, devices):
    rows, cols, depth = snapshot.shape
    shape = jax.ShapeDtypeStruct((rows // 2, SUB, depth), jnp.float32)
    return pl.pallas_call(
        y_edges_kernel,
        in_specs=[pl.BlockSpec(memory_space=pltpu.HBM), VMEM],
        out_specs=[VMEM] * 4,
        out_shape=[
            shape,
            shape,
            jax.ShapeDtypeStruct((devices, LANES), jnp.int32),
            jax.ShapeDtypeStruct((rows, LANES), jnp.int32),
        ],
        scratch_shapes=[
            pltpu.VMEM((rows, SUB, depth), jnp.float32),
            pltpu.VMEM((rows, 2 * SUB, depth), jnp.float32),
            pltpu.SemaphoreType.DMA((2,)),
        ],
        compiler_params=PARAMS,
        name="y_edges",
    )(snapshot, mask)


def row_of(snapshot_ref, left_ref, right_ref, x, lanes, sub):
    rows, cols, _ = snapshot_ref.shape
    half = rows // 2
    left = left_ref[x % half, :, lanes]
    right = right_ref[x % half, :, lanes]
    if x >= half:
        left, right = rolled(left, 4), rolled(right, 4)
    left = jnp.where(sub >= 4, left, 0.0)
    right = jnp.where(sub < 4, right, 0.0)
    inner = [snapshot_ref[x, SUB * k : SUB * (k + 1), lanes] for k in range(cols // SUB)]
    return [left] + inner + [right]


def x_edges_inner_kernel(snapshot_ref, to_before_ref, to_after_ref):
    rows, cols, depth = snapshot_ref.shape

    @pl.loop(0, cols // SUB)
    def _(k):
        inner = pl.ds(pl.multiple_of(SUB * k, SUB), SUB)
        placed = pl.ds(pl.multiple_of(SUB * k + SUB, SUB), SUB)
        for t in range(depth // LANES):
            lanes = slice(t * LANES, (t + 1) * LANES)
            c = {x: [snapshot_ref[x, inner, lanes]] for x in range(rows)}
            for level, (a, b) in enumerate(zip(front_parts(c), back_parts(c))):
                to_before_ref[level, placed, lanes] = a[0]
                to_after_ref[level, placed, lanes] = b[0]


def x_edges_halo_kernel(
    left_ref, right_ref, before_in_ref, after_in_ref, to_before_ref, to_after_ref
):
    half, _, depth = left_ref.shape
    rows = 2 * half
    cols = to_before_ref.shape[1] - 2 * SUB
    sub = sublane()

    @pl.loop(0, depth // LANES)
    def _(t):
        lanes = pl.ds(pl.multiple_of(t * LANES, LANES), LANES)
        for halo_ref, place in ((left_ref, 0), (right_ref, cols + SUB)):
            held = sub >= 4 if place == 0 else sub < 4
            packed = [halo_ref[x, :, lanes] for x in range(half)]
            packed = packed + [rolled(tile, 4) for tile in packed]
            c = {x: [jnp.where(held, packed[x], 0.0)] for x in range(rows)}
            for level, (a, b) in enumerate(zip(front_parts(c), back_parts(c))):
                to_before_ref[level, place : place + SUB, lanes] = a[0]
                to_after_ref[level, place : place + SUB, lanes] = b[0]


def x_edges(snapshot, left, right):
    rows, cols, depth = snapshot.shape
    shape = jax.ShapeDtypeStruct((3, cols + 2 * SUB, depth), jnp.float32)
    before, after = pl.pallas_call(
        x_edges_inner_kernel,
        in_specs=[VMEM],
        out_specs=[VMEM] * 2,
        out_shape=[shape] * 2,
        compiler_params=PARAMS,
        name="x_edges_inner",
    )(snapshot)
    return pl.pallas_call(
        x_edges_halo_kernel,
        in_specs=[VMEM] * 4,
        out_specs=[VMEM] * 2,
        out_shape=[shape] * 2,
        input_output_aliases={2: 0, 3: 1},
        compiler_params=PARAMS,
        name="x_edges_halo",
    )(left, right, before, after)


def main_kernel(
    starts_ref,
    scales_ref,
    snapshot_ref,
    left_ref,
    right_ref,
    before_ref,
    after_ref,
    flags_ref,
    coefficients_hbm_ref,
    packed_ref,
    coefficients_ref,
    ranks,
    sem,
):
    rows, cols, depth = snapshot_ref.shape
    width = depth // LANES
    slots = rows * cols * width
    count = cols // SUB
    per_row = cols * width
    sub = sublane()
    gx, gy = lax.axis_index("gx"), lax.axis_index("gy")
    one, zero = jnp.float32(1.0), jnp.float32(0.0)
    x_left = jnp.where(gx > 0, one, zero)
    x_right = jnp.where(gx < lax.axis_size("gx") - 1, one, zero)
    y_left = jnp.where(gy > 0, one, zero)
    y_right = jnp.where(gy < lax.axis_size("gy") - 1, one, zero)

    scale = [scales_ref[k] for k in range(4)]
    factor = {8: jnp.where(sub % 8 == 0, scale[3], scale[2])}
    factor[4] = jnp.where(sub % 4 == 0, scale[2], scale[1])
    factor[2] = jnp.where(sub % 2 == 0, scale[1], scale[0])
    factor[8] = jnp.where(sub % 4 == 0, factor[8], factor[2])
    factor[4] = jnp.where(sub % 4 == 0, factor[4], factor[2])
    factor[1] = jnp.where(sub % 2 == 0, scale[0], scale[0])
    factor[8] = jnp.where(sub % 2 == 0, factor[8], scale[0])
    factor[4] = jnp.where(sub % 2 == 0, factor[4], scale[0])

    @pl.loop(0, width)
    def _(t):
        lanes = pl.ds(pl.multiple_of(t * LANES, LANES), LANES)

        def load(ref, level):
            return [ref[level, SUB * k : SUB * (k + 1), lanes] for k in range(count + 2)]

        def store(x, row):
            by = 8 if x % 8 == 0 else 4 if x % 4 == 0 else 2 if x % 2 == 0 else 1
            for k in range(count):
                coefficients_ref[x, SUB * k : SUB * (k + 1), lanes] = factor[by] * row[k + 1]

        def step(c, s, beyond, ahead, mine):
            held = sub % s == 0
            half_w, quarter_w = weight(0.5, held), weight(0.25, held)
            end = rows
            c[end] = beyond
            for x in range(s, rows, 2 * s):
                c[x] = [v - half_w * (a + b) for v, a, b in zip(c[x], c[x - s], c[x + s])]
            c[-s] = [v - (half_w * x_left) * a for v, a in zip(ahead, c[0])]
            for x in range(0, rows, 2 * s):
                c[x] = [v + quarter_w * (a + b) for v, a, b in zip(c[x], c[x - s], c[x + s])]
            past = [v + (0.25 * x_right) * a for v, a in zip(mine, c[rows - s])] if mine else None
            return c, past, c[-s]

        def lift(row, s):
            return lift_rows(row, s, sub, y_left, y_right)

        c = {x: row_of(snapshot_ref, left_ref, right_ref, x, lanes, sub) for x in range(rows)}
        c, past, d = step(c, 1, load(after_ref, 0), load(before_ref, 0), load(after_ref, 1))
        for x in range(1, rows, 2):
            store(x, c[x])
        kept = combine(load(before_ref, 1), d, 0.25)
        for x in range(0, rows, 2):
            c[x] = lift(c[x], 1)
        past, kept = lift(past, 1), lift(kept, 1)
        after3, before3 = lift(load(after_ref, 2), 1), lift(load(before_ref, 2), 1)
        mine = [0.875 * v + a for v, a in zip(past, after3)]
        c, past, d = step(c, 2, past, kept, mine)
        for x in range(2, rows, 4):
            store(x, c[x])
        kept = combine(before3, d, 0.25)
        for x in range(0, rows, 4):
            c[x] = lift(c[x], 2)
        past, kept = lift(past, 2), lift(kept, 2)
        c, past, d = step(c, 4, past, kept, None)
        for x in range(4, rows, 8):
            store(x, c[x])
        for x in range(0, rows, 8):
            store(x, lift(c[x], 4))

    copy = pltpu.make_async_copy(coefficients_ref, coefficients_hbm_ref, sem)
    copy.start()
    packed_ref[...] = jnp.zeros_like(packed_ref)
    flags = flags_ref[...]
    source = lax.broadcasted_iota(jnp.int32, (per_row, per_row), 0)
    target = lax.broadcasted_iota(jnp.int32, (per_row, per_row), 1)
    source = source % cols * width + source // cols
    target = target % cols * width + target // cols
    earlier = jnp.where(source < target, one, zero).astype(jnp.bfloat16)
    place = jnp.dot(flags.astype(jnp.bfloat16), earlier, preferred_element_type=jnp.float32)
    ranks[...] = jnp.where(flags > 0, place.astype(jnp.int32), -per_row)
    span = per_row + SUB

    @pl.loop(0, rows)
    def _(x):
        at = starts_ref[x, 0]
        base = pl.multiple_of(lax.shift_left(lax.shift_right_logical(at, 3), 3), SUB)
        wanted = ranks[pl.ds(x, 1), :] + (at - base)
        row_id = lax.broadcasted_iota(jnp.int32, (span, per_row), 0)
        onehot = jnp.where(row_id == wanted, one, zero).astype(jnp.bfloat16)
        values = jnp.concatenate(
            [coefficients_ref[x, :, LANES * t : LANES * (t + 1)] for t in range(width)], axis=0
        )
        high = values.astype(jnp.bfloat16)
        low = (values - high.astype(jnp.float32)).astype(jnp.bfloat16)
        both = jnp.dot(
            onehot, jnp.concatenate([high, low], axis=1), preferred_element_type=jnp.float32
        )
        both = both[:, :LANES] + both[:, LANES:]
        packed_ref[pl.ds(base, SUB), :] += both[:SUB]
        packed_ref[pl.ds(pl.multiple_of(base + SUB, SUB), per_row), :] = both[SUB:]

    packed_ref[slots : slots + TURN, :] = packed_ref[:TURN, :]
    copy.wait()


def main(starts, scales, snapshot, left, right, before, after, flags):
    rows, cols, depth = snapshot.shape
    per_row = flags.shape[1]
    slots = rows * per_row
    return pl.pallas_call(
        main_kernel,
        in_specs=[SMEM] * 2 + [VMEM] * 6,
        out_specs=[pl.BlockSpec(memory_space=pltpu.HBM), VMEM],
        out_shape=[
            jax.ShapeDtypeStruct(snapshot.shape, jnp.float32),
            jax.ShapeDtypeStruct((slots + per_row + SUB, LANES), jnp.float32),
        ],
        scratch_shapes=[
            pltpu.VMEM(snapshot.shape, jnp.float32),
            pltpu.VMEM((rows, per_row), jnp.int32),
            pltpu.SemaphoreType.DMA,
        ],
        compiler_params=PARAMS,
        cost_estimate=pl.CostEstimate(
            flops=2 * 10**9, bytes_accessed=16 * 2**20, transcendentals=0
        ),
        name="lift_and_pack",
    )(starts, scales, snapshot, left, right, before, after, flags)


def turn_kernel(counts_ref, packed_ref, turned_ref):
    slots = turned_ref.shape[0]
    device = lax.axis_index("gx") * lax.axis_size("gy") + lax.axis_index("gy")
    counts = counts_ref[...]
    row_id = lax.broadcasted_iota(jnp.int32, counts.shape, 0)
    earlier = jnp.where(row_id < device, counts, 0)
    offset = jnp.sum(earlier, axis=0, keepdims=True)[0, 0]

    def one(block, carry):
        start = (block * TURN - offset) & (slots - 1)
        to = pl.ds(pl.multiple_of(block * TURN, TURN), TURN)
        turned_ref[to, :] = packed_ref[pl.ds(start, TURN), :]
        return carry

    lax.fori_loop(0, slots // TURN, one, 0, unroll=4)


def turn(counts, packed, slots):
    return pl.pallas_call(
        turn_kernel,
        in_specs=[VMEM] * 2,
        out_specs=VMEM,
        out_shape=jax.ShapeDtypeStruct((slots, LANES), jnp.float32),
        compiler_params=PARAMS,
        name="turn",
    )(counts, packed)


def merge_kernel(counts_ref, arrived_ref, merged_ref):
    devices, share, _ = arrived_ref.shape
    slots = devices * share
    shift = slots.bit_length() - 1
    device = lax.axis_index("gx") * lax.axis_size("gy") + lax.axis_index("gy")
    merged_ref[...] = jnp.zeros_like(merged_ref)
    row_id = lax.broadcasted_iota(jnp.int32, (share, LANES), 0) + device * share

    def one(s, carry):
        start, held = carry
        end = start + counts_ref[s]
        block = lax.shift_right_logical(start, shift)
        rows = arrived_ref[s]
        here = row_id >= (start & (slots - 1))
        held = held + jnp.where(here, rows, 0.0)
        following = jnp.where(here, 0.0, rows)
        merged_ref[jnp.minimum(block + 1, devices - 1)] = following
        merged_ref[block] = held
        crossed = lax.shift_right_logical(end, shift) > block
        return end, jnp.where(crossed, following, held)

    empty = jnp.zeros((share, LANES), jnp.float32)
    lax.fori_loop(0, devices, one, (jnp.int32(0), empty), unroll=4)


def merge(counts, arrived):
    return pl.pallas_call(
        merge_kernel,
        in_specs=[SMEM, VMEM],
        out_specs=VMEM,
        out_shape=jax.ShapeDtypeStruct(arrived.shape, jnp.float32),
        compiler_params=PARAMS,
        name="merge",
    )(counts, arrived)


def on_device(snapshot, keep_mask, exponents):
    rows, cols, depth = snapshot.shape
    width = keep_mask.shape[2]
    devices = lax.axis_size("gx") * lax.axis_size("gy")
    slots = rows * cols * width
    mask = keep_mask.transpose(0, 2, 1)
    to_before, to_after, own_counts, starts = y_edges(snapshot, mask, devices)
    right = shifted(to_before, "gy", -1)
    left = shifted(to_after, "gy", 1)
    counts = lax.all_to_all(own_counts.reshape(devices, 1, LANES), ALL, 0, 0, tiled=True)
    counts = counts.reshape(devices, LANES)
    flags = mask.reshape(rows, cols * width)
    scales = jnp.exp2(exponents.astype(jnp.float32))
    x_before, x_after = x_edges(snapshot, left, right)
    after = shifted(x_before, "gx", -1)
    before = shifted(x_after, "gx", 1)
    coefficients, packed = main(starts, scales, snapshot, left, right, before, after, flags)
    turned = turn(counts, packed, slots)
    share = slots // devices
    arrived = lax.all_to_all(turned.reshape(devices, share, LANES), ALL, 0, 0, tiled=True)
    merged = merge(counts[:, 0], arrived)
    stream = lax.all_to_all(merged, ALL, 0, 0, tiled=True).reshape(slots, LANES)
    return coefficients, stream


def solution(mesh):
    in_specs = (P("gx", "gy", None), P("gx", "gy", None), P())
    out_specs = (P("gx", "gy", None), P(("gx", "gy"), None))
    return jax.shard_map(
        on_device, mesh=mesh, in_specs=in_specs, out_specs=out_specs, check_vma=False
    )
```

```python
import jax
import jax.numpy as jnp
from jax import lax
from jax.experimental import pallas as pl
from jax.experimental.pallas import tpu as pltpu
from jax.sharding import PartitionSpec as P

ALL = ("gx", "gy")
SUB = 8
LANES = 128
PACK_LIMIT = 50 * 2**20
VMEM = pl.BlockSpec(memory_space=pltpu.VMEM)
SMEM = pl.BlockSpec(memory_space=pltpu.SMEM)
PARAMS = pltpu.CompilerParams(vmem_limit_bytes=16 * 2**20)


def shifted(value, axis, steps):
    count = lax.axis_size(axis)
    leading, last = (max(0, -steps), min(count, count - steps))
    return lax.ppermute(value, axis, [(source, source + steps) for source in range(leading, last)])


def sublane():
    return lax.broadcasted_iota(jnp.int32, (SUB, LANES), 0)


def rolled(tile, steps):
    return pltpu.roll(tile, steps % SUB, 0)


def neighbours(tiles, s, sub):
    up = [rolled(t, -s) for t in tiles]
    down = up if 2 * s == SUB else [rolled(t, s) for t in tiles]
    return [
        jnp.where(sub < SUB - s, up[k], up[k + 1]) + jnp.where(sub >= s, down[k], down[k - 1])
        for k in range(1, len(tiles) - 1)
    ]


def weight(value, chosen):
    return jnp.where(chosen, jnp.float32(value), jnp.float32(0.0))


def lift_rows(tiles, s, sub, has_left, has_right):
    odd = weight(0.5, sub % (2 * s) == s)
    even = weight(0.25, sub % (2 * s) == 0)
    left, right = tiles[0], tiles[-1]
    inner = [t - odd * n for t, n in zip(tiles[1:-1], neighbours(tiles, s, sub))]
    ahead = rolled(tiles[1], -s)
    left = left - jnp.where(sub == SUB - s, 0.5 * has_left * ahead, 0.0)
    full = [left] + inner + [right]
    smooth = [t + even * n for t, n in zip(inner, neighbours(full, s, sub))]
    behind = rolled(inner[-1], s)
    if s == 1:
        right = jnp.where(sub == 0, rolled(right, -1) + 0.25 * has_right * behind, right)
        left = left + jnp.where(sub == SUB - 2, 0.25 * rolled(left, -1), 0.0)
    elif s == 2:
        right = jnp.where(
            sub == 0, 0.875 * right + rolled(right, -2) + 0.25 * has_right * behind, right
        )
        left = left + jnp.where(sub == SUB - 4, 0.25 * rolled(left, -2), 0.0)
    return [left] + smooth + [right]


def combine(first, second, scale):
    return [a + scale * b for a, b in zip(first, second)]


def front_parts(c):
    d1, d3, d5 = (combine(c[k], combine(c[k - 1], c[k + 1], 1.0), -0.5) for k in (1, 3, 5))
    c2 = combine(c[2], combine(d1, d3, 1.0), 0.25)
    c4 = combine(c[4], combine(d3, d5, 1.0), 0.25)
    third = [0.25 * (a - 0.5 * b) for a, b in zip(c2, c4)]
    return c[0], combine(c[0], d1, 0.25), third


def back_parts(c):
    d = {k: combine(c[k], combine(c[k - 1], c[k + 1], 1.0), -0.5) for k in (3, 5, 7, 9, 11, 13)}
    e = {k: combine(c[k], combine(d[k - 1], d[k + 1], 1.0), 0.25) for k in (4, 6, 8, 10, 12)}
    d6 = combine(e[6], combine(e[4], e[8], 1.0), -0.5)
    d10 = combine(e[10], combine(e[8], e[12], 1.0), -0.5)
    f8 = combine(e[8], combine(d6, d10, 1.0), 0.25)
    first = combine(c[15], c[14], -0.5)
    second = combine(combine(c[14], d[13], 0.25), e[12], -0.5)
    third = combine(combine(e[12], d10, 0.25), f8, -0.5)
    return first, second, third


def count_kept(mask_ref, counts_ref, starts_ref):
    rows = mask_ref.shape[0]
    kept = mask_ref[:, 0, :]
    for t in range(1, mask_ref.shape[1]):
        kept = kept + mask_ref[:, t, :]
    kept = jnp.sum(kept.astype(jnp.float32), axis=1, keepdims=True)
    kept = jnp.broadcast_to(kept, (rows, LANES))
    shape = (rows, rows)
    later = lax.broadcasted_iota(jnp.int32, shape, 0) > lax.broadcasted_iota(jnp.int32, shape, 1)
    later = jnp.where(later, jnp.float32(1.0), jnp.float32(0.0)).astype(jnp.bfloat16)
    starts = jnp.dot(later, kept.astype(jnp.bfloat16), preferred_element_type=jnp.float32)
    starts_ref[...] = starts.astype(jnp.int32)
    total = (starts[rows - 1 :, :] + kept[rows - 1 :, :]).astype(jnp.int32)
    counts_ref[...] = jnp.broadcast_to(total, counts_ref.shape)


def y_edges_kernel(snapshot_ref, to_before_ref, to_after_ref):
    rows, cols, depth = snapshot_ref.shape
    half = rows // 2
    sub = sublane()
    zero = jnp.zeros((SUB, LANES), jnp.float32)

    def before(x, lanes):
        v = snapshot_ref[x, :SUB, lanes]
        d1 = v - weight(0.5, sub % 2 == 1) * (rolled(v, -1) + rolled(v, 1))
        c2 = d1 + 0.25 * (rolled(d1, -1) + rolled(d1, 1))
        second = rolled(v, 1) + 0.25 * d1
        third = 0.25 * (c2 - 0.5 * rolled(c2, -2))
        return jnp.where(
            sub == 0, v, jnp.where(sub == 1, second, jnp.where(sub == 2, third, 0.0))
        )

    def after(x, lanes):
        last = [snapshot_ref[x, cols - n * SUB : cols - (n - 1) * SUB, lanes] for n in (2, 1)]
        v = [zero] + last + [zero]
        odd = weight(0.5, sub % 2 == 1)
        d = [zero] + [t - odd * n for t, n in zip(v[1:-1], neighbours(v, 1, sub))] + [zero]
        even = weight(0.25, sub % 2 == 0)
        e = [zero] + [t + even * n for t, n in zip(d[1:-1], neighbours(d, 1, sub))] + [zero]
        odd = weight(0.5, sub % 4 == 2)
        f = [zero] + [t - odd * n for t, n in zip(e[1:-1], neighbours(e, 2, sub))] + [zero]
        even = weight(0.25, sub % 4 == 0)
        g = [t + even * n for t, n in zip(f[1:-1], neighbours(f, 2, sub))]
        first = d[2]
        second = v[2] + 0.25 * rolled(d[2], 1) - 0.5 * rolled(e[2], 2)
        third = e[2] + 0.25 * rolled(f[2], 2) - 0.5 * rolled(g[1], 4)
        return jnp.where(
            sub == 7, first, jnp.where(sub == 6, second, jnp.where(sub == 4, third, 0.0))
        )

    @pl.loop(0, half)
    def _(x):
        for t in range(depth // LANES):
            lanes = slice(t * LANES, (t + 1) * LANES)
            to_before_ref[x, :, lanes] = before(x, lanes) + rolled(before(x + half, lanes), 4)
            to_after_ref[x, :, lanes] = after(x, lanes) + rolled(after(x + half, lanes), 4)


def y_edges(snapshot):
    rows, cols, depth = snapshot.shape
    shape = jax.ShapeDtypeStruct((rows // 2, SUB, depth), jnp.float32)
    return pl.pallas_call(
        y_edges_kernel,
        in_specs=[VMEM],
        out_specs=[VMEM] * 2,
        out_shape=[shape] * 2,
        compiler_params=PARAMS,
        name="y_edges",
    )(snapshot)


def row_of(snapshot_ref, left_ref, right_ref, x, lanes, sub):
    rows, cols, _ = snapshot_ref.shape
    half = rows // 2
    left = left_ref[x % half, :, lanes]
    right = right_ref[x % half, :, lanes]
    if x >= half:
        left, right = rolled(left, 4), rolled(right, 4)
    left = jnp.where(sub >= 4, left, 0.0)
    right = jnp.where(sub < 4, right, 0.0)
    inner = [snapshot_ref[x, SUB * k : SUB * (k + 1), lanes] for k in range(cols // SUB)]
    return [left] + inner + [right]


def x_edges_inner_kernel(
    snapshot_ref, mask_ref, to_before_ref, to_after_ref, counts_ref, starts_ref
):
    rows, cols, depth = snapshot_ref.shape
    count_kept(mask_ref, counts_ref, starts_ref)

    @pl.loop(0, cols // SUB)
    def _(k):
        inner = pl.ds(pl.multiple_of(SUB * k, SUB), SUB)
        placed = pl.ds(pl.multiple_of(SUB * k + SUB, SUB), SUB)
        for t in range(depth // LANES):
            lanes = slice(t * LANES, (t + 1) * LANES)
            c = {x: [snapshot_ref[x, inner, lanes]] for x in range(rows)}
            for level, (a, b) in enumerate(zip(front_parts(c), back_parts(c))):
                to_before_ref[level, placed, lanes] = a[0]
                to_after_ref[level, placed, lanes] = b[0]


def x_edges_halo_kernel(
    left_ref, right_ref, before_in_ref, after_in_ref, to_before_ref, to_after_ref
):
    half, _, depth = left_ref.shape
    rows = 2 * half
    cols = to_before_ref.shape[1] - 2 * SUB
    sub = sublane()

    @pl.loop(0, depth // LANES)
    def _(t):
        lanes = pl.ds(pl.multiple_of(t * LANES, LANES), LANES)
        for halo_ref, place in ((left_ref, 0), (right_ref, cols + SUB)):
            held = sub >= 4 if place == 0 else sub < 4
            packed = [halo_ref[x, :, lanes] for x in range(half)]
            packed = packed + [rolled(tile, 4) for tile in packed]
            c = {x: [jnp.where(held, packed[x], 0.0)] for x in range(rows)}
            for level, (a, b) in enumerate(zip(front_parts(c), back_parts(c))):
                to_before_ref[level, place : place + SUB, lanes] = a[0]
                to_after_ref[level, place : place + SUB, lanes] = b[0]


def x_edges_inner(snapshot, mask, devices):
    rows, cols, depth = snapshot.shape
    shape = jax.ShapeDtypeStruct((3, cols + 2 * SUB, depth), jnp.float32)
    return pl.pallas_call(
        x_edges_inner_kernel,
        in_specs=[VMEM] * 2,
        out_specs=[VMEM] * 4,
        out_shape=[
            shape,
            shape,
            jax.ShapeDtypeStruct((devices, LANES), jnp.int32),
            jax.ShapeDtypeStruct((rows, LANES), jnp.int32),
        ],
        compiler_params=PARAMS,
        name="x_edges_inner",
    )(snapshot, mask)


def x_edges_halo(left, right, before, after):
    shape = jax.ShapeDtypeStruct(before.shape, jnp.float32)
    return pl.pallas_call(
        x_edges_halo_kernel,
        in_specs=[VMEM] * 4,
        out_specs=[VMEM] * 2,
        out_shape=[shape] * 2,
        input_output_aliases={2: 0, 3: 1},
        compiler_params=PARAMS,
        name="x_edges_halo",
    )(left, right, before, after)


def lift_kernel(
    scales_ref,
    snapshot_ref,
    left_ref,
    right_ref,
    before_ref,
    after_ref,
    coefficients_hbm_ref,
    coefficients_ref,
    sems,
):
    rows, cols, depth = snapshot_ref.shape
    width = depth // LANES
    count = cols // SUB
    sub = sublane()
    gx, gy = lax.axis_index("gx"), lax.axis_index("gy")
    one, zero = jnp.float32(1.0), jnp.float32(0.0)
    x_left = jnp.where(gx > 0, one, zero)
    x_right = jnp.where(gx < lax.axis_size("gx") - 1, one, zero)
    y_left = jnp.where(gy > 0, one, zero)
    y_right = jnp.where(gy < lax.axis_size("gy") - 1, one, zero)

    scale = [scales_ref[k] for k in range(4)]
    factor = {8: jnp.where(sub % 8 == 0, scale[3], scale[2])}
    factor[4] = jnp.where(sub % 4 == 0, scale[2], scale[1])
    factor[2] = jnp.where(sub % 2 == 0, scale[1], scale[0])
    factor[8] = jnp.where(sub % 4 == 0, factor[8], factor[2])
    factor[4] = jnp.where(sub % 4 == 0, factor[4], factor[2])
    factor[1] = jnp.where(sub % 2 == 0, scale[0], scale[0])
    factor[8] = jnp.where(sub % 2 == 0, factor[8], scale[0])
    factor[4] = jnp.where(sub % 2 == 0, factor[4], scale[0])

    def write(t):
        lanes = pl.ds(pl.multiple_of(t * LANES, LANES), LANES)
        return pltpu.make_async_copy(
            coefficients_ref.at[:, :, lanes], coefficients_hbm_ref.at[:, :, lanes], sems.at[t]
        )

    @pl.loop(0, width)
    def _(t):
        lanes = pl.ds(pl.multiple_of(t * LANES, LANES), LANES)

        def load(ref, level):
            return [ref[level, SUB * k : SUB * (k + 1), lanes] for k in range(count + 2)]

        def store(x, row):
            by = 8 if x % 8 == 0 else 4 if x % 4 == 0 else 2 if x % 2 == 0 else 1
            for k in range(count):
                coefficients_ref[x, SUB * k : SUB * (k + 1), lanes] = factor[by] * row[k + 1]

        def step(c, s, beyond, ahead, mine):
            held = sub % s == 0
            half_w, quarter_w = weight(0.5, held), weight(0.25, held)
            end = rows
            c[end] = beyond
            for x in range(s, rows, 2 * s):
                c[x] = [v - half_w * (a + b) for v, a, b in zip(c[x], c[x - s], c[x + s])]
            c[-s] = [v - (half_w * x_left) * a for v, a in zip(ahead, c[0])]
            for x in range(0, rows, 2 * s):
                c[x] = [v + quarter_w * (a + b) for v, a, b in zip(c[x], c[x - s], c[x + s])]
            past = [v + (0.25 * x_right) * a for v, a in zip(mine, c[rows - s])] if mine else None
            return c, past, c[-s]

        def lift(row, s):
            return lift_rows(row, s, sub, y_left, y_right)

        c = {x: row_of(snapshot_ref, left_ref, right_ref, x, lanes, sub) for x in range(rows)}
        c, past, d = step(c, 1, load(after_ref, 0), load(before_ref, 0), load(after_ref, 1))
        for x in range(1, rows, 2):
            store(x, c[x])
        kept = combine(load(before_ref, 1), d, 0.25)
        for x in range(0, rows, 2):
            c[x] = lift(c[x], 1)
        past, kept = lift(past, 1), lift(kept, 1)
        after3, before3 = lift(load(after_ref, 2), 1), lift(load(before_ref, 2), 1)
        mine = [0.875 * v + a for v, a in zip(past, after3)]
        c, past, d = step(c, 2, past, kept, mine)
        for x in range(2, rows, 4):
            store(x, c[x])
        kept = combine(before3, d, 0.25)
        for x in range(0, rows, 4):
            c[x] = lift(c[x], 2)
        past, kept = lift(past, 2), lift(kept, 2)
        c, past, d = step(c, 4, past, kept, None)
        for x in range(4, rows, 8):
            store(x, c[x])
        for x in range(0, rows, 8):
            store(x, lift(c[x], 4))
        write(t).start()

    @pl.loop(0, width)
    def _(t):
        write(t).wait()


def lift(scales, snapshot, left, right, before, after):
    return pl.pallas_call(
        lift_kernel,
        in_specs=[SMEM] + [VMEM] * 5,
        out_specs=pl.BlockSpec(memory_space=pltpu.HBM),
        out_shape=jax.ShapeDtypeStruct(snapshot.shape, jnp.float32),
        scratch_shapes=[
            pltpu.VMEM(snapshot.shape, jnp.float32),
            pltpu.SemaphoreType.DMA((snapshot.shape[2] // LANES,)),
        ],
        compiler_params=PARAMS,
        cost_estimate=pl.CostEstimate(
            flops=2 * 10**9, bytes_accessed=16 * 2**20, transcendentals=0
        ),
        name="lift",
    )(scales, snapshot, left, right, before, after)


def pack_kernel(
    table_ref,
    starts_ref,
    coefficients_hbm_ref,
    flags_ref,
    packed_ref,
    counts_ref,
    coefficients_ref,
    buffer,
    ranks,
    sems,
):
    rows, cols, depth = coefficients_ref.shape
    width = depth // LANES
    slots = rows * cols * width
    per_row = cols * width
    one, zero = jnp.float32(1.0), jnp.float32(0.0)
    group = rows // sems.shape[0]

    def read(part):
        part = pl.ds(part * group, group)
        return pltpu.make_async_copy(
            coefficients_hbm_ref.at[part], coefficients_ref.at[part], sems.at[part.start // group]
        )

    for part in range(rows // group):
        read(part).start()

    device = lax.axis_index("gx") * lax.axis_size("gy") + lax.axis_index("gy")
    table = table_ref[...]
    row_id = lax.broadcasted_iota(jnp.int32, table.shape, 0)
    lane_id = lax.broadcasted_iota(jnp.int32, table.shape, 1)
    offset = jnp.sum(jnp.where(row_id < device, table, 0), axis=0, keepdims=True)[0, 0]
    counts_ref[...] = jnp.sum(jnp.where(row_id == lane_id, table, 0), axis=0, keepdims=True)
    buffer[...] = jnp.zeros_like(buffer)
    flags = flags_ref[...]
    source = lax.broadcasted_iota(jnp.int32, (per_row, per_row), 0)
    target = lax.broadcasted_iota(jnp.int32, (per_row, per_row), 1)
    source = source % cols * width + source // cols
    target = target % cols * width + target // cols
    earlier = jnp.where(source < target, one, zero).astype(jnp.bfloat16)
    place = jnp.dot(flags.astype(jnp.bfloat16), earlier, preferred_element_type=jnp.float32)
    ranks[...] = jnp.where(flags > 0, place.astype(jnp.int32), -per_row)
    span = per_row + SUB

    def place_row(x):
        at = (offset + starts_ref[x, 0]) & (slots - 1)
        base = pl.multiple_of(lax.shift_left(lax.shift_right_logical(at, 3), 3), SUB)
        wanted = ranks[x : x + 1, :] + (at - base)
        row_id = lax.broadcasted_iota(jnp.int32, (span, per_row), 0)
        onehot = jnp.where(row_id == wanted, one, zero).astype(jnp.bfloat16)
        values = jnp.concatenate(
            [coefficients_ref[x, :, LANES * t : LANES * (t + 1)] for t in range(width)], axis=0
        )
        high = values.astype(jnp.bfloat16)
        low = (values - high.astype(jnp.float32)).astype(jnp.bfloat16)
        both = jnp.dot(
            onehot, jnp.concatenate([high, low], axis=1), preferred_element_type=jnp.float32
        )
        buffer[pl.ds(base, span), :] += both[:, :LANES] + both[:, LANES:]

    for part in range(rows // group):
        read(part).wait()
        for x in range(part * group, part * group + group):
            place_row(x)

    packed_ref[span:, :] = buffer[span:slots, :]
    packed_ref[:span, :] = buffer[:span, :] + buffer[slots:, :]


def pack(table, starts, coefficients, flags):
    rows, cols, depth = coefficients.shape
    per_row = flags.shape[1]
    slots = rows * per_row
    return pl.pallas_call(
        pack_kernel,
        in_specs=[VMEM, SMEM, pl.BlockSpec(memory_space=pltpu.HBM), VMEM],
        out_specs=[VMEM] * 2,
        out_shape=[
            jax.ShapeDtypeStruct((slots, LANES), jnp.float32),
            jax.ShapeDtypeStruct((1, table.shape[0]), jnp.int32),
        ],
        scratch_shapes=[
            pltpu.VMEM(coefficients.shape, jnp.float32),
            pltpu.VMEM((slots + per_row + SUB, LANES), jnp.float32),
            pltpu.VMEM((rows, per_row), jnp.int32),
            pltpu.SemaphoreType.DMA((4,)),
        ],
        compiler_params=pltpu.CompilerParams(vmem_limit_bytes=PACK_LIMIT),
        name="pack",
    )(table, starts, coefficients, flags)


def merge_kernel(counts_ref, arrived_ref, merged_ref):
    devices, share, _ = arrived_ref.shape
    slots = devices * share
    shift = slots.bit_length() - 1
    device = lax.axis_index("gx") * lax.axis_size("gy") + lax.axis_index("gy")
    merged_ref[...] = jnp.zeros_like(merged_ref)
    row_id = lax.broadcasted_iota(jnp.int32, (share, LANES), 0) + device * share

    def one(s, carry):
        start, held = carry
        end = start + counts_ref[0, s]
        block = lax.shift_right_logical(start, shift)
        rows = arrived_ref[s]
        here = row_id >= (start & (slots - 1))
        held = held + jnp.where(here, rows, 0.0)
        following = jnp.where(here, 0.0, rows)
        merged_ref[jnp.minimum(block + 1, devices - 1)] = following
        merged_ref[block] = held
        crossed = lax.shift_right_logical(end, shift) > block
        return end, jnp.where(crossed, following, held)

    empty = jnp.zeros((share, LANES), jnp.float32)
    lax.fori_loop(0, devices, one, (jnp.int32(0), empty), unroll=4)


def merge(counts, arrived):
    return pl.pallas_call(
        merge_kernel,
        in_specs=[SMEM, VMEM],
        out_specs=VMEM,
        out_shape=jax.ShapeDtypeStruct(arrived.shape, jnp.float32),
        compiler_params=PARAMS,
        name="merge",
    )(counts, arrived)


def on_device(snapshot, keep_mask, exponents):
    rows, cols, depth = snapshot.shape
    width = keep_mask.shape[2]
    devices = lax.axis_size("gx") * lax.axis_size("gy")
    slots = rows * cols * width
    mask = keep_mask.transpose(0, 2, 1)
    to_before, to_after = y_edges(snapshot)
    right = shifted(to_before, "gy", -1)
    left = shifted(to_after, "gy", 1)
    x_before, x_after, own_counts, starts = x_edges_inner(snapshot, mask, devices)
    table = lax.all_to_all(own_counts.reshape(devices, 1, LANES), ALL, 0, 0, tiled=True)
    table = table.reshape(devices, LANES)
    flags = mask.reshape(rows, cols * width)
    scales = jnp.exp2(exponents.astype(jnp.float32))
    x_before, x_after = x_edges_halo(left, right, x_before, x_after)
    after = shifted(x_before, "gx", -1)
    before = shifted(x_after, "gx", 1)
    coefficients = lift(scales, snapshot, left, right, before, after)
    packed, counts = pack(table, starts, coefficients, flags)
    share = slots // devices
    arrived = lax.all_to_all(packed.reshape(devices, share, LANES), ALL, 0, 0, tiled=True)
    merged = merge(counts, arrived)
    stream = lax.all_to_all(merged, ALL, 0, 0, tiled=True).reshape(slots, LANES)
    return coefficients, stream


def solution(mesh):
    in_specs = (P("gx", "gy", None), P("gx", "gy", None), P())
    out_specs = (P("gx", "gy", None), P(("gx", "gy"), None))
    return jax.shard_map(
        on_device, mesh=mesh, in_specs=in_specs, out_specs=out_specs, check_vma=False
    )
```

```python
import jax
import jax.numpy as jnp
from jax import lax
from jax.experimental import pallas as pl
from jax.experimental.pallas import tpu as pltpu
from jax.sharding import PartitionSpec as P

ALL = ("gx", "gy")
SUB = 8
LANES = 128
PACK_LIMIT = 50 * 2**20
VMEM = pl.BlockSpec(memory_space=pltpu.VMEM)
SMEM = pl.BlockSpec(memory_space=pltpu.SMEM)
PARAMS = pltpu.CompilerParams(vmem_limit_bytes=16 * 2**20)


def shifted(value, axis, steps):
    count = lax.axis_size(axis)
    leading, last = (max(0, -steps), min(count, count - steps))
    return lax.ppermute(value, axis, [(source, source + steps) for source in range(leading, last)])


def sublane():
    return lax.broadcasted_iota(jnp.int32, (SUB, LANES), 0)


def rolled(tile, steps):
    return pltpu.roll(tile, steps % SUB, 0)


def neighbours(tiles, s, sub):
    up = [rolled(t, -s) for t in tiles]
    down = up if 2 * s == SUB else [rolled(t, s) for t in tiles]
    return [
        jnp.where(sub < SUB - s, up[k], up[k + 1]) + jnp.where(sub >= s, down[k], down[k - 1])
        for k in range(1, len(tiles) - 1)
    ]


def around_odd(tiles, s, sub):
    up = [rolled(t, -s) for t in tiles]
    if 2 * s == SUB:
        return [a + b for a, b in zip(up[:-1], up[1:])]
    return [
        jnp.where(sub == SUB - s, up[k + 1], up[k]) + rolled(tiles[k], s)
        for k in range(len(tiles) - 1)
    ]


def around_even(tiles, s, sub):
    down = [rolled(t, s) for t in tiles]
    if 2 * s == SUB:
        return [a + b for a, b in zip(down[1:], down[:-1])]
    return [
        jnp.where(sub == 0, down[k - 1], down[k]) + rolled(tiles[k], -s)
        for k in range(1, len(tiles))
    ]


def weight(value, chosen):
    return jnp.where(chosen, jnp.float32(value), jnp.float32(0.0))


def lift_rows(tiles, s, sub, has_left, has_right):
    odd = weight(0.5, sub % (2 * s) == s)
    even = weight(0.25, sub % (2 * s) == 0)
    left, right = tiles[0], tiles[-1]
    inner = [t - odd * n for t, n in zip(tiles[1:-1], around_odd(tiles[1:], s, sub))]
    ahead = rolled(tiles[1], -s)
    left = left - jnp.where(sub == SUB - s, 0.5 * has_left * ahead, 0.0)
    smooth = [t + even * n for t, n in zip(inner, around_even([left] + inner, s, sub))]
    behind = rolled(inner[-1], s)
    if s == 1:
        right = jnp.where(sub == 0, rolled(right, -1) + 0.25 * has_right * behind, right)
        left = left + jnp.where(sub == SUB - 2, 0.25 * rolled(left, -1), 0.0)
    elif s == 2:
        right = jnp.where(
            sub == 0, 0.875 * right + rolled(right, -2) + 0.25 * has_right * behind, right
        )
        left = left + jnp.where(sub == SUB - 4, 0.25 * rolled(left, -2), 0.0)
    return [left] + smooth + [right]


def combine(first, second, scale):
    return [a + scale * b for a, b in zip(first, second)]


def front_parts(c):
    d1, d3, d5 = (combine(c[k], combine(c[k - 1], c[k + 1], 1.0), -0.5) for k in (1, 3, 5))
    c2 = combine(c[2], combine(d1, d3, 1.0), 0.25)
    c4 = combine(c[4], combine(d3, d5, 1.0), 0.25)
    third = [0.25 * (a - 0.5 * b) for a, b in zip(c2, c4)]
    return c[0], combine(c[0], d1, 0.25), third


def back_parts(c):
    d = {k: combine(c[k], combine(c[k - 1], c[k + 1], 1.0), -0.5) for k in (3, 5, 7, 9, 11, 13)}
    e = {k: combine(c[k], combine(d[k - 1], d[k + 1], 1.0), 0.25) for k in (4, 6, 8, 10, 12)}
    d6 = combine(e[6], combine(e[4], e[8], 1.0), -0.5)
    d10 = combine(e[10], combine(e[8], e[12], 1.0), -0.5)
    f8 = combine(e[8], combine(d6, d10, 1.0), 0.25)
    first = combine(c[15], c[14], -0.5)
    second = combine(combine(c[14], d[13], 0.25), e[12], -0.5)
    third = combine(combine(e[12], d10, 0.25), f8, -0.5)
    return first, second, third


def count_kept(mask_ref, counts_ref, starts_ref):
    rows = mask_ref.shape[0]
    kept = mask_ref[:, 0, :]
    for t in range(1, mask_ref.shape[1]):
        kept = kept + mask_ref[:, t, :]
    kept = jnp.sum(kept.astype(jnp.float32), axis=1, keepdims=True)
    kept = jnp.broadcast_to(kept, (rows, LANES))
    shape = (rows, rows)
    later = lax.broadcasted_iota(jnp.int32, shape, 0) > lax.broadcasted_iota(jnp.int32, shape, 1)
    later = jnp.where(later, jnp.float32(1.0), jnp.float32(0.0)).astype(jnp.bfloat16)
    starts = jnp.dot(later, kept.astype(jnp.bfloat16), preferred_element_type=jnp.float32)
    starts_ref[...] = starts.astype(jnp.int32)
    total = (starts[rows - 1 :, :] + kept[rows - 1 :, :]).astype(jnp.int32)
    counts_ref[...] = jnp.broadcast_to(total, counts_ref.shape)


def y_edges_kernel(snapshot_ref, to_before_ref, to_after_ref):
    rows, cols, depth = snapshot_ref.shape
    half = rows // 2
    sub = sublane()
    zero = jnp.zeros((SUB, LANES), jnp.float32)

    def before(x, lanes):
        v = snapshot_ref[x, :SUB, lanes]
        d1 = v - weight(0.5, sub % 2 == 1) * (rolled(v, -1) + rolled(v, 1))
        c2 = d1 + 0.25 * (rolled(d1, -1) + rolled(d1, 1))
        second = rolled(v, 1) + 0.25 * d1
        third = 0.25 * (c2 - 0.5 * rolled(c2, -2))
        return jnp.where(
            sub == 0, v, jnp.where(sub == 1, second, jnp.where(sub == 2, third, 0.0))
        )

    def after(x, lanes):
        last = [snapshot_ref[x, cols - n * SUB : cols - (n - 1) * SUB, lanes] for n in (2, 1)]
        v = [zero] + last + [zero]
        odd = weight(0.5, sub % 2 == 1)
        d = [zero] + [t - odd * n for t, n in zip(v[1:-1], neighbours(v, 1, sub))] + [zero]
        even = weight(0.25, sub % 2 == 0)
        e = [zero] + [t + even * n for t, n in zip(d[1:-1], neighbours(d, 1, sub))] + [zero]
        odd = weight(0.5, sub % 4 == 2)
        f = [zero] + [t - odd * n for t, n in zip(e[1:-1], neighbours(e, 2, sub))] + [zero]
        even = weight(0.25, sub % 4 == 0)
        g = [t + even * n for t, n in zip(f[1:-1], neighbours(f, 2, sub))]
        first = d[2]
        second = v[2] + 0.25 * rolled(d[2], 1) - 0.5 * rolled(e[2], 2)
        third = e[2] + 0.25 * rolled(f[2], 2) - 0.5 * rolled(g[1], 4)
        return jnp.where(
            sub == 7, first, jnp.where(sub == 6, second, jnp.where(sub == 4, third, 0.0))
        )

    @pl.loop(0, half)
    def _(x):
        for t in range(depth // LANES):
            lanes = slice(t * LANES, (t + 1) * LANES)
            to_before_ref[x, :, lanes] = before(x, lanes) + rolled(before(x + half, lanes), 4)
            to_after_ref[x, :, lanes] = after(x, lanes) + rolled(after(x + half, lanes), 4)


def y_edges(snapshot):
    rows, cols, depth = snapshot.shape
    shape = jax.ShapeDtypeStruct((rows // 2, SUB, depth), jnp.float32)
    return pl.pallas_call(
        y_edges_kernel,
        in_specs=[VMEM],
        out_specs=[VMEM] * 2,
        out_shape=[shape] * 2,
        compiler_params=PARAMS,
        name="y_edges",
    )(snapshot)


def x_edges_inner_kernel(
    snapshot_ref, mask_ref, to_before_ref, to_after_ref, counts_ref, starts_ref
):
    rows, cols, depth = snapshot_ref.shape
    count_kept(mask_ref, counts_ref, starts_ref)

    @pl.loop(0, cols // SUB)
    def _(k):
        inner = pl.ds(pl.multiple_of(SUB * k, SUB), SUB)
        placed = pl.ds(pl.multiple_of(SUB * k + SUB, SUB), SUB)
        for t in range(depth // LANES):
            lanes = slice(t * LANES, (t + 1) * LANES)
            c = {x: [snapshot_ref[x, inner, lanes]] for x in range(rows)}
            for level, (a, b) in enumerate(zip(front_parts(c), back_parts(c))):
                to_before_ref[level, placed, lanes] = a[0]
                to_after_ref[level, placed, lanes] = b[0]


def x_edges_halo_kernel(
    left_ref, right_ref, before_in_ref, after_in_ref, to_before_ref, to_after_ref
):
    half, _, depth = left_ref.shape
    rows = 2 * half
    cols = to_before_ref.shape[1] - 2 * SUB
    sub = sublane()

    @pl.loop(0, depth // LANES)
    def _(t):
        lanes = pl.ds(pl.multiple_of(t * LANES, LANES), LANES)
        for halo_ref, place in ((left_ref, 0), (right_ref, cols + SUB)):
            held = sub >= 4 if place == 0 else sub < 4
            packed = [halo_ref[x, :, lanes] for x in range(half)]
            packed = packed + [rolled(tile, 4) for tile in packed]
            c = {x: [jnp.where(held, packed[x], 0.0)] for x in range(rows)}
            for level, (a, b) in enumerate(zip(front_parts(c), back_parts(c))):
                to_before_ref[level, place : place + SUB, lanes] = a[0]
                to_after_ref[level, place : place + SUB, lanes] = b[0]


def x_edges_inner(snapshot, mask, devices):
    rows, cols, depth = snapshot.shape
    shape = jax.ShapeDtypeStruct((3, cols + 2 * SUB, depth), jnp.float32)
    return pl.pallas_call(
        x_edges_inner_kernel,
        in_specs=[VMEM] * 2,
        out_specs=[VMEM] * 4,
        out_shape=[
            shape,
            shape,
            jax.ShapeDtypeStruct((devices, LANES), jnp.int32),
            jax.ShapeDtypeStruct((rows, LANES), jnp.int32),
        ],
        compiler_params=PARAMS,
        name="x_edges_inner",
    )(snapshot, mask)


def x_edges_halo(left, right, before, after):
    shape = jax.ShapeDtypeStruct(before.shape, jnp.float32)
    return pl.pallas_call(
        x_edges_halo_kernel,
        in_specs=[VMEM] * 4,
        out_specs=[VMEM] * 2,
        out_shape=[shape] * 2,
        input_output_aliases={2: 0, 3: 1},
        compiler_params=PARAMS,
        name="x_edges_halo",
    )(left, right, before, after)


def lift_kernel(
    scales_ref,
    snapshot_ref,
    left_ref,
    right_ref,
    before_ref,
    after_ref,
    coefficients_hbm_ref,
    front_ref,
    back_ref,
    work,
    sems,
):
    rows, cols, depth = snapshot_ref.shape
    width = depth // LANES
    count = cols // SUB
    sub = sublane()
    gx, gy = lax.axis_index("gx"), lax.axis_index("gy")
    one, zero = jnp.float32(1.0), jnp.float32(0.0)
    x_left = jnp.where(gx > 0, one, zero)
    x_right = jnp.where(gx < lax.axis_size("gx") - 1, one, zero)
    y_left = jnp.where(gy > 0, one, zero)
    y_right = jnp.where(gy < lax.axis_size("gy") - 1, one, zero)

    scale = [scales_ref[k] for k in range(4)]
    factor = {8: jnp.where(sub % 8 == 0, scale[3], scale[2])}
    factor[4] = jnp.where(sub % 4 == 0, scale[2], scale[1])
    factor[2] = jnp.where(sub % 2 == 0, scale[1], scale[0])
    factor[8] = jnp.where(sub % 4 == 0, factor[8], factor[2])
    factor[4] = jnp.where(sub % 4 == 0, factor[4], factor[2])
    factor[1] = jnp.where(sub % 2 == 0, scale[0], scale[0])
    factor[8] = jnp.where(sub % 2 == 0, factor[8], scale[0])
    factor[4] = jnp.where(sub % 2 == 0, factor[4], scale[0])

    half = rows // 2
    past_at, kept_at, after_at, before_at = range(half, half + 4)

    def write(t):
        lanes = pl.ds(pl.multiple_of(t * LANES, LANES), LANES)
        return [
            pltpu.make_async_copy(
                ref.at[:, :, lanes], coefficients_hbm_ref.at[at : at + half, :, lanes], sems.at[t, i]
            )
            for i, (ref, at) in enumerate(((front_ref, 0), (back_ref, half)))
        ]

    @pl.loop(0, width)
    def _(t):
        lanes = pl.ds(pl.multiple_of(t * LANES, LANES), LANES)

        def span(k):
            return slice(SUB * k, SUB * (k + 1))

        def store(x, k, tile):
            if 1 <= k <= count:
                by = 8 if x % 8 == 0 else 4 if x % 4 == 0 else 2 if x % 2 == 0 else 1
                ref = front_ref if x < half else back_ref
                ref[x % half, span(k - 1), lanes] = factor[by] * tile

        def entry(x, k):
            if 1 <= k <= count:
                return snapshot_ref[x, span(k - 1), lanes]
            tile = (left_ref if k == 0 else right_ref)[x % half, :, lanes]
            tile = rolled(tile, 4) if x >= half else tile
            return jnp.where(sub >= 4 if k == 0 else sub < 4, tile, 0.0)

        def step(c, s, beyond, ahead):
            held = sub % s == 0
            half_w, quarter_w = (weight(0.5, held), weight(0.25, held)) if s > 1 else (0.5, 0.25)
            c[rows] = beyond
            for x in range(s, rows, 2 * s):
                c[x] = c[x] - half_w * (c[x - s] + c[x + s])
            c[-s] = ahead - (half_w * x_left) * c[0]
            for x in range(0, rows, 2 * s):
                c[x] = c[x] + quarter_w * (c[x - s] + c[x + s])
            return c

        def lift_row(source, target, s):
            row = [source(k) for k in range(count + 2)]
            for k, tile in enumerate(lift_rows(row, s, sub, y_left, y_right)):
                target(k, tile)

        def held_at(at):
            return lambda k: work[at, span(k)]

        def put_at(at):
            def put(k, tile):
                work[at, span(k)] = tile

            return put

        for k in range(count + 2):
            c = {x: entry(x, k) for x in range(rows)}
            c = step(c, 1, after_ref[0, span(k), lanes], before_ref[0, span(k), lanes])
            for x in range(1, rows, 2):
                store(x, k, c[x])
            for x in range(0, rows, 2):
                work[x // 2, span(k)] = c[x]
            work[past_at, span(k)] = after_ref[1, span(k), lanes] + (0.25 * x_right) * c[rows - 1]
            work[kept_at, span(k)] = before_ref[1, span(k), lanes] + 0.25 * c[-1]
        for at in range(half + 2):
            lift_row(held_at(at), put_at(at), 1)
        lift_row(lambda k: after_ref[2, span(k), lanes], put_at(after_at), 1)
        lift_row(lambda k: before_ref[2, span(k), lanes], put_at(before_at), 1)
        for k in range(count + 2):
            c = {x: work[x // 2, span(k)] for x in range(0, rows, 2)}
            past = work[past_at, span(k)]
            c = step(c, 2, past, work[kept_at, span(k)])
            for x in range(2, rows, 4):
                store(x, k, c[x])
            for x in range(0, rows, 4):
                work[x // 2, span(k)] = c[x]
            mine = 0.875 * past + work[after_at, span(k)]
            work[past_at, span(k)] = mine + (0.25 * x_right) * c[rows - 2]
            work[kept_at, span(k)] = work[before_at, span(k)] + 0.25 * c[-2]
        for at in [x // 2 for x in range(0, rows, 4)] + [past_at, kept_at]:
            lift_row(held_at(at), put_at(at), 2)
        for k in range(count + 2):
            c = {x: work[x // 2, span(k)] for x in range(0, rows, 4)}
            c = step(c, 4, work[past_at, span(k)], work[kept_at, span(k)])
            for x in range(4, rows, 8):
                store(x, k, c[x])
            for x in range(0, rows, 8):
                work[x // 2, span(k)] = c[x]
        for x in range(0, rows, 8):
            lift_row(held_at(x // 2), lambda k, tile, x=x: store(x, k, tile), 4)
        for copy in write(t):
            copy.start()

    @pl.loop(0, width)
    def _(t):
        for copy in write(t):
            copy.wait()


def lift(scales, snapshot, left, right, before, after):
    rows, cols, depth = snapshot.shape
    return pl.pallas_call(
        lift_kernel,
        in_specs=[SMEM] + [VMEM] * 5,
        out_specs=[pl.BlockSpec(memory_space=pltpu.HBM), VMEM],
        out_shape=[
            jax.ShapeDtypeStruct(snapshot.shape, jnp.float32),
            jax.ShapeDtypeStruct((rows // 2, cols, depth), jnp.float32),
        ],
        scratch_shapes=[
            pltpu.VMEM((rows // 2, cols, depth), jnp.float32),
            pltpu.VMEM((rows // 2 + 4, cols + 2 * SUB, LANES), jnp.float32),
            pltpu.SemaphoreType.DMA((depth // LANES, 2)),
        ],
        compiler_params=PARAMS,
        cost_estimate=pl.CostEstimate(
            flops=2 * 10**9, bytes_accessed=16 * 2**20, transcendentals=0
        ),
        name="lift",
    )(scales, snapshot, left, right, before, after)


def pack_kernel(
    table_ref,
    starts_ref,
    coefficients_hbm_ref,
    front_ref,
    flags_ref,
    packed_ref,
    counts_ref,
    back_ref,
    buffer,
    ranks,
    sems,
):
    half, cols, depth = front_ref.shape
    rows = 2 * half
    width = depth // LANES
    slots = rows * cols * width
    per_row = cols * width
    one, zero = jnp.float32(1.0), jnp.float32(0.0)
    parts = sems.shape[0]
    group = half // parts
    copies = [
        pltpu.make_async_copy(
            coefficients_hbm_ref.at[half + group * part : half + group * (part + 1)],
            back_ref.at[group * part : group * (part + 1)],
            sems.at[part],
        )
        for part in range(parts)
    ]
    for copy in copies:
        copy.start()

    device = lax.axis_index("gx") * lax.axis_size("gy") + lax.axis_index("gy")
    table = table_ref[...]
    row_id = lax.broadcasted_iota(jnp.int32, table.shape, 0)
    lane_id = lax.broadcasted_iota(jnp.int32, table.shape, 1)
    offset = jnp.sum(jnp.where(row_id < device, table, 0), axis=0, keepdims=True)[0, 0]
    counts_ref[...] = jnp.sum(jnp.where(row_id == lane_id, table, 0), axis=0, keepdims=True)
    buffer[...] = jnp.zeros_like(buffer)
    flags = flags_ref[...]
    source = lax.broadcasted_iota(jnp.int32, (per_row, per_row), 0)
    target = lax.broadcasted_iota(jnp.int32, (per_row, per_row), 1)
    source = source % cols * width + source // cols
    target = target % cols * width + target // cols
    earlier = jnp.where(source < target, one, zero).astype(jnp.bfloat16)
    place = jnp.dot(flags.astype(jnp.bfloat16), earlier, preferred_element_type=jnp.float32)
    ranks[...] = jnp.where(flags > 0, place.astype(jnp.int32), -per_row)
    span = per_row + SUB

    def place_row(x):
        ref = front_ref if x < half else back_ref
        at = (offset + starts_ref[x, 0]) & (slots - 1)
        base = pl.multiple_of(lax.shift_left(lax.shift_right_logical(at, 3), 3), SUB)
        wanted = ranks[x : x + 1, :] + (at - base)
        row_id = lax.broadcasted_iota(jnp.int32, (span, per_row), 0)
        onehot = jnp.where(row_id == wanted, one, zero).astype(jnp.bfloat16)
        values = jnp.concatenate(
            [ref[x % half, :, LANES * t : LANES * (t + 1)] for t in range(width)], axis=0
        )
        high = values.astype(jnp.bfloat16)
        low = (values - high.astype(jnp.float32)).astype(jnp.bfloat16)
        both = jnp.dot(
            onehot, jnp.concatenate([high, low], axis=1), preferred_element_type=jnp.float32
        )
        buffer[pl.ds(base, span), :] += both[:, :LANES] + both[:, LANES:]

    for x in range(rows):
        if x >= half and x % group == 0:
            copies[(x - half) // group].wait()
        place_row(x)

    packed_ref[span:, :] = buffer[span:slots, :]
    packed_ref[:span, :] = buffer[:span, :] + buffer[slots:, :]


def pack(table, starts, coefficients, front, flags):
    rows, cols, depth = coefficients.shape
    per_row = flags.shape[1]
    slots = rows * per_row
    return pl.pallas_call(
        pack_kernel,
        in_specs=[VMEM, SMEM, pl.BlockSpec(memory_space=pltpu.HBM), VMEM, VMEM],
        out_specs=[VMEM] * 2,
        out_shape=[
            jax.ShapeDtypeStruct((slots, LANES), jnp.float32),
            jax.ShapeDtypeStruct((1, table.shape[0]), jnp.int32),
        ],
        scratch_shapes=[
            pltpu.VMEM((rows // 2, cols, depth), jnp.float32),
            pltpu.VMEM((slots + per_row + SUB, LANES), jnp.float32),
            pltpu.VMEM((rows, per_row), jnp.int32),
            pltpu.SemaphoreType.DMA((2,)),
        ],
        compiler_params=pltpu.CompilerParams(vmem_limit_bytes=PACK_LIMIT),
        name="pack",
    )(table, starts, coefficients, front, flags)


def merge_kernel(counts_ref, arrived_ref, merged_ref):
    devices, share, _ = arrived_ref.shape
    slots = devices * share
    shift = slots.bit_length() - 1
    device = lax.axis_index("gx") * lax.axis_size("gy") + lax.axis_index("gy")
    merged_ref[...] = jnp.zeros_like(merged_ref)
    row_id = lax.broadcasted_iota(jnp.int32, (share, LANES), 0) + device * share

    def one(s, carry):
        start, held = carry
        end = start + counts_ref[0, s]
        block = lax.shift_right_logical(start, shift)
        rows = arrived_ref[s]
        here = row_id >= (start & (slots - 1))
        held = held + jnp.where(here, rows, 0.0)
        following = jnp.where(here, 0.0, rows)
        merged_ref[jnp.minimum(block + 1, devices - 1)] = following
        merged_ref[block] = held
        crossed = lax.shift_right_logical(end, shift) > block
        return end, jnp.where(crossed, following, held)

    empty = jnp.zeros((share, LANES), jnp.float32)
    lax.fori_loop(0, devices, one, (jnp.int32(0), empty), unroll=4)


def merge(counts, arrived):
    return pl.pallas_call(
        merge_kernel,
        in_specs=[SMEM, VMEM],
        out_specs=VMEM,
        out_shape=jax.ShapeDtypeStruct(arrived.shape, jnp.float32),
        compiler_params=PARAMS,
        name="merge",
    )(counts, arrived)


def on_device(snapshot, keep_mask, exponents):
    rows, cols, depth = snapshot.shape
    width = keep_mask.shape[2]
    devices = lax.axis_size("gx") * lax.axis_size("gy")
    slots = rows * cols * width
    mask = keep_mask.transpose(0, 2, 1)
    to_before, to_after = y_edges(snapshot)
    right = shifted(to_before, "gy", -1)
    left = shifted(to_after, "gy", 1)
    x_before, x_after, own_counts, starts = x_edges_inner(snapshot, mask, devices)
    table = lax.all_to_all(own_counts.reshape(devices, 1, LANES), ALL, 0, 0, tiled=True)
    table = table.reshape(devices, LANES)
    flags = mask.reshape(rows, cols * width)
    scales = jnp.exp2(exponents.astype(jnp.float32))
    x_before, x_after = x_edges_halo(left, right, x_before, x_after)
    after = shifted(x_before, "gx", -1)
    before = shifted(x_after, "gx", 1)
    coefficients, front = lift(scales, snapshot, left, right, before, after)
    packed, counts = pack(table, starts, coefficients, front, flags)
    share = slots // devices
    arrived = lax.all_to_all(packed.reshape(devices, share, LANES), ALL, 0, 0, tiled=True)
    merged = merge(counts, arrived)
    stream = lax.all_to_all(merged, ALL, 0, 0, tiled=True).reshape(slots, LANES)
    return coefficients, stream


def solution(mesh):
    in_specs = (P("gx", "gy", None), P("gx", "gy", None), P())
    out_specs = (P("gx", "gy", None), P(("gx", "gy"), None))
    return jax.shard_map(
        on_device, mesh=mesh, in_specs=in_specs, out_specs=out_specs, check_vma=False
    )
```

```python
import jax
import jax.numpy as jnp
from jax import lax
from jax.experimental import pallas as pl
from jax.experimental.pallas import tpu as pltpu
from jax.sharding import PartitionSpec as P

ALL = ("gx", "gy")
SUB = 8
LANES = 128
PACK_LIMIT = 50 * 2**20
VMEM = pl.BlockSpec(memory_space=pltpu.VMEM)
SMEM = pl.BlockSpec(memory_space=pltpu.SMEM)
PARAMS = pltpu.CompilerParams(vmem_limit_bytes=16 * 2**20)


def pairs_exchange(first, second, axis, ring):
    count = lax.axis_size(axis)
    inner = [(k, k ^ 1) for k in range(count)]
    outer = [(k, k + 1 if k % 2 else k - 1) for k in range(0 if ring else 1, count - (not ring))]
    outer = [(a % count, b % count) for a, b in outer]
    return lax.ppermute(first, axis, inner), lax.ppermute(second, axis, outer)


def is_even(axis):
    return lax.axis_index(axis) % 2 == 0


def sublane():
    return lax.broadcasted_iota(jnp.int32, (SUB, LANES), 0)


def rolled(tile, steps):
    return pltpu.roll(tile, steps % SUB, 0)


def neighbours(tiles, s, sub):
    up = [rolled(t, -s) for t in tiles]
    down = up if 2 * s == SUB else [rolled(t, s) for t in tiles]
    return [
        jnp.where(sub < SUB - s, up[k], up[k + 1]) + jnp.where(sub >= s, down[k], down[k - 1])
        for k in range(1, len(tiles) - 1)
    ]


def around_odd(tiles, s, sub):
    up = [rolled(t, -s) for t in tiles]
    if 2 * s == SUB:
        return [a + b for a, b in zip(up[:-1], up[1:])]
    return [
        jnp.where(sub == SUB - s, up[k + 1], up[k]) + rolled(tiles[k], s)
        for k in range(len(tiles) - 1)
    ]


def around_even(tiles, s, sub):
    down = [rolled(t, s) for t in tiles]
    if 2 * s == SUB:
        return [a + b for a, b in zip(down[1:], down[:-1])]
    return [
        jnp.where(sub == 0, down[k - 1], down[k]) + rolled(tiles[k], -s)
        for k in range(1, len(tiles))
    ]


def weight(value, chosen):
    return jnp.where(chosen, jnp.float32(value), jnp.float32(0.0))


def lift_rows(tiles, s, sub, has_left, has_right):
    odd = weight(0.5, sub % (2 * s) == s)
    even = weight(0.25, sub % (2 * s) == 0)
    left, right = tiles[0], tiles[-1]
    inner = [t - odd * n for t, n in zip(tiles[1:-1], around_odd(tiles[1:], s, sub))]
    ahead = rolled(tiles[1], -s)
    left = left - jnp.where(sub == SUB - s, 0.5 * has_left * ahead, 0.0)
    smooth = [t + even * n for t, n in zip(inner, around_even([left] + inner, s, sub))]
    behind = rolled(inner[-1], s)
    if s == 1:
        right = jnp.where(sub == 0, rolled(right, -1) + 0.25 * has_right * behind, right)
        left = left + jnp.where(sub == SUB - 2, 0.25 * rolled(left, -1), 0.0)
    elif s == 2:
        right = jnp.where(
            sub == 0, 0.875 * right + rolled(right, -2) + 0.25 * has_right * behind, right
        )
        left = left + jnp.where(sub == SUB - 4, 0.25 * rolled(left, -2), 0.0)
    return [left] + smooth + [right]


def combine(first, second, scale):
    return [a + scale * b for a, b in zip(first, second)]


def front_parts(c):
    d1, d3, d5 = (combine(c[k], combine(c[k - 1], c[k + 1], 1.0), -0.5) for k in (1, 3, 5))
    c2 = combine(c[2], combine(d1, d3, 1.0), 0.25)
    c4 = combine(c[4], combine(d3, d5, 1.0), 0.25)
    third = [0.25 * (a - 0.5 * b) for a, b in zip(c2, c4)]
    return c[0], combine(c[0], d1, 0.25), third


def back_parts(c):
    d = {k: combine(c[k], combine(c[k - 1], c[k + 1], 1.0), -0.5) for k in (3, 5, 7, 9, 11, 13)}
    e = {k: combine(c[k], combine(d[k - 1], d[k + 1], 1.0), 0.25) for k in (4, 6, 8, 10, 12)}
    d6 = combine(e[6], combine(e[4], e[8], 1.0), -0.5)
    d10 = combine(e[10], combine(e[8], e[12], 1.0), -0.5)
    f8 = combine(e[8], combine(d6, d10, 1.0), 0.25)
    first = combine(c[15], c[14], -0.5)
    second = combine(combine(c[14], d[13], 0.25), e[12], -0.5)
    third = combine(combine(e[12], d10, 0.25), f8, -0.5)
    return first, second, third


def count_kept(mask_ref, counts_ref, starts_ref):
    rows = mask_ref.shape[0]
    kept = mask_ref[:, 0, :]
    for t in range(1, mask_ref.shape[1]):
        kept = kept + mask_ref[:, t, :]
    kept = jnp.sum(kept.astype(jnp.float32), axis=1, keepdims=True)
    kept = jnp.broadcast_to(kept, (rows, LANES))
    shape = (rows, rows)
    later = lax.broadcasted_iota(jnp.int32, shape, 0) > lax.broadcasted_iota(jnp.int32, shape, 1)
    later = jnp.where(later, jnp.float32(1.0), jnp.float32(0.0)).astype(jnp.bfloat16)
    starts = jnp.dot(later, kept.astype(jnp.bfloat16), preferred_element_type=jnp.float32)
    starts_ref[...] = starts.astype(jnp.int32)
    total = (starts[rows - 1 :, :] + kept[rows - 1 :, :]).astype(jnp.int32)
    counts_ref[...] = jnp.broadcast_to(total, counts_ref.shape)


def y_edges_kernel(snapshot_ref, inner_ref, outer_ref):
    rows, cols, depth = snapshot_ref.shape
    half = rows // 2
    even_gy = is_even("gy")
    sub = sublane()
    zero = jnp.zeros((SUB, LANES), jnp.float32)

    def before(x, lanes):
        v = snapshot_ref[x, :SUB, lanes]
        d1 = v - weight(0.5, sub % 2 == 1) * (rolled(v, -1) + rolled(v, 1))
        c2 = d1 + 0.25 * (rolled(d1, -1) + rolled(d1, 1))
        second = rolled(v, 1) + 0.25 * d1
        third = 0.25 * (c2 - 0.5 * rolled(c2, -2))
        return jnp.where(
            sub == 0, v, jnp.where(sub == 1, second, jnp.where(sub == 2, third, 0.0))
        )

    def after(x, lanes):
        last = [snapshot_ref[x, cols - n * SUB : cols - (n - 1) * SUB, lanes] for n in (2, 1)]
        v = [zero] + last + [zero]
        odd = weight(0.5, sub % 2 == 1)
        d = [zero] + [t - odd * n for t, n in zip(v[1:-1], neighbours(v, 1, sub))] + [zero]
        even = weight(0.25, sub % 2 == 0)
        e = [zero] + [t + even * n for t, n in zip(d[1:-1], neighbours(d, 1, sub))] + [zero]
        odd = weight(0.5, sub % 4 == 2)
        f = [zero] + [t - odd * n for t, n in zip(e[1:-1], neighbours(e, 2, sub))] + [zero]
        even = weight(0.25, sub % 4 == 0)
        g = [t + even * n for t, n in zip(f[1:-1], neighbours(f, 2, sub))]
        first = d[2]
        second = v[2] + 0.25 * rolled(d[2], 1) - 0.5 * rolled(e[2], 2)
        third = e[2] + 0.25 * rolled(f[2], 2) - 0.5 * rolled(g[1], 4)
        return jnp.where(
            sub == 7, first, jnp.where(sub == 6, second, jnp.where(sub == 4, third, 0.0))
        )

    @pl.loop(0, half)
    def _(x):
        for t in range(depth // LANES):
            lanes = slice(t * LANES, (t + 1) * LANES)
            to_before = before(x, lanes) + rolled(before(x + half, lanes), 4)
            to_after = after(x, lanes) + rolled(after(x + half, lanes), 4)
            inner_ref[x, :, lanes] = jnp.where(even_gy, to_after, to_before)
            outer_ref[x, :, lanes] = jnp.where(even_gy, to_before, to_after)


def y_edges(snapshot):
    rows, cols, depth = snapshot.shape
    shape = jax.ShapeDtypeStruct((rows // 2, SUB, depth), jnp.float32)
    return pl.pallas_call(
        y_edges_kernel,
        in_specs=[VMEM],
        out_specs=[VMEM] * 2,
        out_shape=[shape] * 2,
        compiler_params=PARAMS,
        name="y_edges",
    )(snapshot)


def x_edges_inner_kernel(
    snapshot_ref, mask_ref, inner_ref, outer_ref, counts_ref, starts_ref
):
    rows, cols, depth = snapshot_ref.shape
    even_gx = is_even("gx")
    count_kept(mask_ref, counts_ref, starts_ref)

    @pl.loop(0, cols // SUB)
    def _(k):
        here = pl.ds(pl.multiple_of(SUB * k, SUB), SUB)
        placed = pl.ds(pl.multiple_of(SUB * k + SUB, SUB), SUB)
        for t in range(depth // LANES):
            lanes = slice(t * LANES, (t + 1) * LANES)
            c = {x: [snapshot_ref[x, here, lanes]] for x in range(rows)}
            for level, (a, b) in enumerate(zip(front_parts(c), back_parts(c))):
                inner_ref[level, placed, lanes] = jnp.where(even_gx, b[0], a[0])
                outer_ref[level, placed, lanes] = jnp.where(even_gx, a[0], b[0])


def x_edges_halo_kernel(y_inner_ref, y_outer_ref, _, __, inner_ref, outer_ref):
    half, _, depth = y_inner_ref.shape
    rows = 2 * half
    cols = inner_ref.shape[1] - 2 * SUB
    sub = sublane()
    gy = lax.axis_index("gy")
    even_gy, even_gx = is_even("gy"), is_even("gx")

    @pl.loop(0, depth // LANES)
    def _(t):
        lanes = pl.ds(pl.multiple_of(t * LANES, LANES), LANES)
        for place in (0, cols + SUB):
            if place == 0:
                held, swap = (sub >= 4) & (gy > 0), even_gy
            else:
                held, swap = (sub < 4) & (gy < lax.axis_size("gy") - 1), ~even_gy
            packed = [
                jnp.where(swap, y_outer_ref[x, :, lanes], y_inner_ref[x, :, lanes])
                for x in range(half)
            ]
            packed = packed + [rolled(tile, 4) for tile in packed]
            c = {x: [jnp.where(held, packed[x], 0.0)] for x in range(rows)}
            for level, (a, b) in enumerate(zip(front_parts(c), back_parts(c))):
                inner_ref[level, place : place + SUB, lanes] = jnp.where(even_gx, b[0], a[0])
                outer_ref[level, place : place + SUB, lanes] = jnp.where(even_gx, a[0], b[0])


def x_edges_inner(snapshot, mask, devices):
    rows, cols, depth = snapshot.shape
    shape = jax.ShapeDtypeStruct((3, cols + 2 * SUB, depth), jnp.float32)
    return pl.pallas_call(
        x_edges_inner_kernel,
        in_specs=[VMEM] * 2,
        out_specs=[VMEM] * 4,
        out_shape=[
            shape,
            shape,
            jax.ShapeDtypeStruct((devices, LANES), jnp.int32),
            jax.ShapeDtypeStruct((rows, LANES), jnp.int32),
        ],
        compiler_params=PARAMS,
        name="x_edges_inner",
    )(snapshot, mask)


def x_edges_halo(y_inner, y_outer, x_inner, x_outer):
    shape = jax.ShapeDtypeStruct(x_inner.shape, jnp.float32)
    return pl.pallas_call(
        x_edges_halo_kernel,
        in_specs=[VMEM] * 4,
        out_specs=[VMEM] * 2,
        out_shape=[shape] * 2,
        input_output_aliases={2: 0, 3: 1},
        compiler_params=PARAMS,
        name="x_edges_halo",
    )(y_inner, y_outer, x_inner, x_outer)


def lift_kernel(
    scales_ref,
    snapshot_ref,
    y_inner_ref,
    y_outer_ref,
    x_inner_ref,
    x_outer_ref,
    coefficients_hbm_ref,
    front_ref,
    back_ref,
    work,
    sems,
):
    rows, cols, depth = snapshot_ref.shape
    width = depth // LANES
    count = cols // SUB
    sub = sublane()
    gx, gy = lax.axis_index("gx"), lax.axis_index("gy")
    one, zero = jnp.float32(1.0), jnp.float32(0.0)
    x_left = jnp.where(gx > 0, one, zero)
    x_right = jnp.where(gx < lax.axis_size("gx") - 1, one, zero)
    y_left = jnp.where(gy > 0, one, zero)
    y_right = jnp.where(gy < lax.axis_size("gy") - 1, one, zero)

    scale = [scales_ref[k] for k in range(4)]
    factor = {8: jnp.where(sub % 8 == 0, scale[3], scale[2])}
    factor[4] = jnp.where(sub % 4 == 0, scale[2], scale[1])
    factor[2] = jnp.where(sub % 2 == 0, scale[1], scale[0])
    factor[8] = jnp.where(sub % 4 == 0, factor[8], factor[2])
    factor[4] = jnp.where(sub % 4 == 0, factor[4], factor[2])
    factor[1] = jnp.where(sub % 2 == 0, scale[0], scale[0])
    factor[8] = jnp.where(sub % 2 == 0, factor[8], scale[0])
    factor[4] = jnp.where(sub % 2 == 0, factor[4], scale[0])

    even_gx, even_gy = is_even("gx"), is_even("gy")
    left_held = (sub >= 4) & (gy > 0)
    right_held = (sub < 4) & (gy < lax.axis_size("gy") - 1)
    half = rows // 2
    past_at, kept_at, after_at, before_at = range(half, half + 4)

    def write(t):
        lanes = pl.ds(pl.multiple_of(t * LANES, LANES), LANES)
        return [
            pltpu.make_async_copy(
                ref.at[:, :, lanes], coefficients_hbm_ref.at[at : at + half, :, lanes], sems.at[t, i]
            )
            for i, (ref, at) in enumerate(((front_ref, 0), (back_ref, half)))
        ]

    @pl.loop(0, width)
    def _(t):
        lanes = pl.ds(pl.multiple_of(t * LANES, LANES), LANES)

        def span(k):
            return slice(SUB * k, SUB * (k + 1))

        def store(x, k, tile):
            if 1 <= k <= count:
                by = 8 if x % 8 == 0 else 4 if x % 4 == 0 else 2 if x % 2 == 0 else 1
                ref = front_ref if x < half else back_ref
                ref[x % half, span(k - 1), lanes] = factor[by] * tile

        def entry(x, k):
            if 1 <= k <= count:
                return snapshot_ref[x, span(k - 1), lanes]
            inner, outer = y_inner_ref[x % half, :, lanes], y_outer_ref[x % half, :, lanes]
            tile = jnp.where(even_gy if k == 0 else ~even_gy, outer, inner)
            tile = rolled(tile, 4) if x >= half else tile
            return jnp.where(left_held if k == 0 else right_held, tile, 0.0)

        def before(level, k):
            inner, outer = x_inner_ref[level, span(k), lanes], x_outer_ref[level, span(k), lanes]
            return jnp.where(even_gx, outer, inner)

        def after(level, k):
            inner, outer = x_inner_ref[level, span(k), lanes], x_outer_ref[level, span(k), lanes]
            return jnp.where(even_gx, inner, outer)

        def step(c, s, beyond, ahead):
            held = sub % s == 0
            half_w, quarter_w = (weight(0.5, held), weight(0.25, held)) if s > 1 else (0.5, 0.25)
            c[rows] = beyond
            for x in range(s, rows, 2 * s):
                c[x] = c[x] - half_w * (c[x - s] + c[x + s])
            c[-s] = ahead - (half_w * x_left) * c[0]
            for x in range(0, rows, 2 * s):
                c[x] = c[x] + quarter_w * (c[x - s] + c[x + s])
            return c

        def lift_row(source, target, s):
            row = [source(k) for k in range(count + 2)]
            for k, tile in enumerate(lift_rows(row, s, sub, y_left, y_right)):
                target(k, tile)

        def held_at(at):
            return lambda k: work[at, span(k)]

        def put_at(at):
            def put(k, tile):
                work[at, span(k)] = tile

            return put

        for k in range(count + 2):
            c = {x: entry(x, k) for x in range(rows)}
            c = step(c, 1, after(0, k), before(0, k))
            for x in range(1, rows, 2):
                store(x, k, c[x])
            for x in range(0, rows, 2):
                work[x // 2, span(k)] = c[x]
            work[past_at, span(k)] = after(1, k) + (0.25 * x_right) * c[rows - 1]
            work[kept_at, span(k)] = before(1, k) + 0.25 * c[-1]
        for at in range(half + 2):
            lift_row(held_at(at), put_at(at), 1)
        lift_row(lambda k: after(2, k), put_at(after_at), 1)
        lift_row(lambda k: before(2, k), put_at(before_at), 1)
        for k in range(count + 2):
            c = {x: work[x // 2, span(k)] for x in range(0, rows, 2)}
            past = work[past_at, span(k)]
            c = step(c, 2, past, work[kept_at, span(k)])
            for x in range(2, rows, 4):
                store(x, k, c[x])
            for x in range(0, rows, 4):
                work[x // 2, span(k)] = c[x]
            mine = 0.875 * past + work[after_at, span(k)]
            work[past_at, span(k)] = mine + (0.25 * x_right) * c[rows - 2]
            work[kept_at, span(k)] = work[before_at, span(k)] + 0.25 * c[-2]
        for at in [x // 2 for x in range(0, rows, 4)] + [past_at, kept_at]:
            lift_row(held_at(at), put_at(at), 2)
        for k in range(count + 2):
            c = {x: work[x // 2, span(k)] for x in range(0, rows, 4)}
            c = step(c, 4, work[past_at, span(k)], work[kept_at, span(k)])
            for x in range(4, rows, 8):
                store(x, k, c[x])
            for x in range(0, rows, 8):
                work[x // 2, span(k)] = c[x]
        for x in range(0, rows, 8):
            lift_row(held_at(x // 2), lambda k, tile, x=x: store(x, k, tile), 4)
        for copy in write(t):
            copy.start()

    @pl.loop(0, width)
    def _(t):
        for copy in write(t):
            copy.wait()


def lift(scales, snapshot, y_inner, y_outer, x_inner, x_outer):
    rows, cols, depth = snapshot.shape
    return pl.pallas_call(
        lift_kernel,
        in_specs=[SMEM] + [VMEM] * 5,
        out_specs=[pl.BlockSpec(memory_space=pltpu.HBM), VMEM],
        out_shape=[
            jax.ShapeDtypeStruct(snapshot.shape, jnp.float32),
            jax.ShapeDtypeStruct((rows // 2, cols, depth), jnp.float32),
        ],
        scratch_shapes=[
            pltpu.VMEM((rows // 2, cols, depth), jnp.float32),
            pltpu.VMEM((rows // 2 + 4, cols + 2 * SUB, LANES), jnp.float32),
            pltpu.SemaphoreType.DMA((depth // LANES, 2)),
        ],
        compiler_params=PARAMS,
        cost_estimate=pl.CostEstimate(
            flops=2 * 10**9, bytes_accessed=16 * 2**20, transcendentals=0
        ),
        name="lift",
    )(scales, snapshot, y_inner, y_outer, x_inner, x_outer)


def pack_kernel(
    table_ref,
    starts_ref,
    coefficients_hbm_ref,
    front_ref,
    flags_ref,
    packed_ref,
    counts_ref,
    back_ref,
    buffer,
    ranks,
    sems,
):
    half, cols, depth = front_ref.shape
    rows = 2 * half
    width = depth // LANES
    slots = rows * cols * width
    per_row = cols * width
    one, zero = jnp.float32(1.0), jnp.float32(0.0)
    parts = sems.shape[0]
    group = half // parts
    copies = [
        pltpu.make_async_copy(
            coefficients_hbm_ref.at[half + group * part : half + group * (part + 1)],
            back_ref.at[group * part : group * (part + 1)],
            sems.at[part],
        )
        for part in range(parts)
    ]
    for copy in copies:
        copy.start()

    device = lax.axis_index("gx") * lax.axis_size("gy") + lax.axis_index("gy")
    table = table_ref[...]
    row_id = lax.broadcasted_iota(jnp.int32, table.shape, 0)
    lane_id = lax.broadcasted_iota(jnp.int32, table.shape, 1)
    offset = jnp.sum(jnp.where(row_id < device, table, 0), axis=0, keepdims=True)[0, 0]
    counts_ref[...] = jnp.sum(jnp.where(row_id == lane_id, table, 0), axis=0, keepdims=True)
    buffer[...] = jnp.zeros_like(buffer)
    flags = flags_ref[...]
    source = lax.broadcasted_iota(jnp.int32, (per_row, per_row), 0)
    target = lax.broadcasted_iota(jnp.int32, (per_row, per_row), 1)
    source = source % cols * width + source // cols
    target = target % cols * width + target // cols
    earlier = jnp.where(source < target, one, zero).astype(jnp.bfloat16)
    place = jnp.dot(flags.astype(jnp.bfloat16), earlier, preferred_element_type=jnp.float32)
    ranks[...] = jnp.where(flags > 0, place.astype(jnp.int32), -per_row)
    span = per_row + SUB

    def place_row(x):
        ref = front_ref if x < half else back_ref
        at = (offset + starts_ref[x, 0]) & (slots - 1)
        base = pl.multiple_of(lax.shift_left(lax.shift_right_logical(at, 3), 3), SUB)
        wanted = ranks[x : x + 1, :] + (at - base)
        row_id = lax.broadcasted_iota(jnp.int32, (span, per_row), 0)
        onehot = jnp.where(row_id == wanted, one, zero).astype(jnp.bfloat16)
        values = jnp.concatenate(
            [ref[x % half, :, LANES * t : LANES * (t + 1)] for t in range(width)], axis=0
        )
        high = values.astype(jnp.bfloat16)
        low = (values - high.astype(jnp.float32)).astype(jnp.bfloat16)
        both = jnp.dot(
            onehot, jnp.concatenate([high, low], axis=1), preferred_element_type=jnp.float32
        )
        buffer[pl.ds(base, span), :] += both[:, :LANES] + both[:, LANES:]

    for x in range(rows):
        if x >= half and x % group == 0:
            copies[(x - half) // group].wait()
        place_row(x)

    packed_ref[span:, :] = buffer[span:slots, :]
    packed_ref[:span, :] = buffer[:span, :] + buffer[slots:, :]


def pack(table, starts, coefficients, front, flags):
    rows, cols, depth = coefficients.shape
    per_row = flags.shape[1]
    slots = rows * per_row
    return pl.pallas_call(
        pack_kernel,
        in_specs=[VMEM, SMEM, pl.BlockSpec(memory_space=pltpu.HBM), VMEM, VMEM],
        out_specs=[VMEM] * 2,
        out_shape=[
            jax.ShapeDtypeStruct((slots, LANES), jnp.float32),
            jax.ShapeDtypeStruct((1, table.shape[0]), jnp.int32),
        ],
        scratch_shapes=[
            pltpu.VMEM((rows // 2, cols, depth), jnp.float32),
            pltpu.VMEM((slots + per_row + SUB, LANES), jnp.float32),
            pltpu.VMEM((rows, per_row), jnp.int32),
            pltpu.SemaphoreType.DMA((2,)),
        ],
        compiler_params=pltpu.CompilerParams(vmem_limit_bytes=PACK_LIMIT),
        name="pack",
    )(table, starts, coefficients, front, flags)


def merge_kernel(counts_ref, arrived_ref, merged_ref):
    devices, share, _ = arrived_ref.shape
    slots = devices * share
    shift = slots.bit_length() - 1
    device = lax.axis_index("gx") * lax.axis_size("gy") + lax.axis_index("gy")
    merged_ref[...] = jnp.zeros_like(merged_ref)
    row_id = lax.broadcasted_iota(jnp.int32, (share, LANES), 0) + device * share

    def one(s, carry):
        start, held = carry
        end = start + counts_ref[0, s]
        block = lax.shift_right_logical(start, shift)
        rows = arrived_ref[s]
        here = row_id >= (start & (slots - 1))
        held = held + jnp.where(here, rows, 0.0)
        following = jnp.where(here, 0.0, rows)
        merged_ref[jnp.minimum(block + 1, devices - 1)] = following
        merged_ref[block] = held
        crossed = lax.shift_right_logical(end, shift) > block
        return end, jnp.where(crossed, following, held)

    empty = jnp.zeros((share, LANES), jnp.float32)
    lax.fori_loop(0, devices, one, (jnp.int32(0), empty), unroll=4)


def merge(counts, arrived):
    return pl.pallas_call(
        merge_kernel,
        in_specs=[SMEM, VMEM],
        out_specs=VMEM,
        out_shape=jax.ShapeDtypeStruct(arrived.shape, jnp.float32),
        compiler_params=PARAMS,
        name="merge",
    )(counts, arrived)


def on_device(snapshot, keep_mask, exponents):
    rows, cols, depth = snapshot.shape
    width = keep_mask.shape[2]
    devices = lax.axis_size("gx") * lax.axis_size("gy")
    slots = rows * cols * width
    mask = keep_mask.transpose(0, 2, 1)
    y_halo = pairs_exchange(*y_edges(snapshot), "gy", ring=True)
    x_inner, x_outer, own_counts, starts = x_edges_inner(snapshot, mask, devices)
    table = lax.all_to_all(own_counts.reshape(devices, 1, LANES), ALL, 0, 0, tiled=True)
    table = table.reshape(devices, LANES)
    flags = mask.reshape(rows, cols * width)
    scales = jnp.exp2(exponents.astype(jnp.float32))
    x_halo = pairs_exchange(*x_edges_halo(*y_halo, x_inner, x_outer), "gx", ring=False)
    coefficients, front = lift(scales, snapshot, *y_halo, *x_halo)
    packed, counts = pack(table, starts, coefficients, front, flags)
    share = slots // devices
    arrived = lax.all_to_all(packed.reshape(devices, share, LANES), ALL, 0, 0, tiled=True)
    merged = merge(counts, arrived)
    stream = lax.all_to_all(merged, ALL, 0, 0, tiled=True).reshape(slots, LANES)
    return coefficients, stream


def solution(mesh):
    in_specs = (P("gx", "gy", None), P("gx", "gy", None), P())
    out_specs = (P("gx", "gy", None), P(("gx", "gy"), None))
    return jax.shard_map(
        on_device, mesh=mesh, in_specs=in_specs, out_specs=out_specs, check_vma=False
    )
```

```python
import jax
import jax.numpy as jnp
from jax import lax
from jax.experimental import pallas as pl
from jax.experimental.pallas import tpu as pltpu
from jax.sharding import PartitionSpec as P

ALL = ("gx", "gy")
SUB = 8
LANES = 128
EDGE_LIMIT = 50 * 2**20
PACK_LIMIT = 50 * 2**20
VMEM = pl.BlockSpec(memory_space=pltpu.VMEM)
SMEM = pl.BlockSpec(memory_space=pltpu.SMEM)
PARAMS = pltpu.CompilerParams(vmem_limit_bytes=16 * 2**20)


def pairs_exchange(first, second, axis, ring):
    count = lax.axis_size(axis)
    inner = [(k, k ^ 1) for k in range(count)]
    outer = [(k, k + 1 if k % 2 else k - 1) for k in range(0 if ring else 1, count - (not ring))]
    outer = [(a % count, b % count) for a, b in outer]
    return lax.ppermute(first, axis, inner), lax.ppermute(second, axis, outer)


def is_even(axis):
    return lax.axis_index(axis) % 2 == 0


def sublane():
    return lax.broadcasted_iota(jnp.int32, (SUB, LANES), 0)


def rolled(tile, steps):
    return pltpu.roll(tile, steps % SUB, 0)


def neighbours(tiles, s, sub):
    up = [rolled(t, -s) for t in tiles]
    down = up if 2 * s == SUB else [rolled(t, s) for t in tiles]
    return [
        jnp.where(sub < SUB - s, up[k], up[k + 1]) + jnp.where(sub >= s, down[k], down[k - 1])
        for k in range(1, len(tiles) - 1)
    ]


def around_odd(tiles, s, sub):
    up = [rolled(t, -s) for t in tiles]
    if 2 * s == SUB:
        return [a + b for a, b in zip(up[:-1], up[1:])]
    return [
        jnp.where(sub == SUB - s, up[k + 1], up[k]) + rolled(tiles[k], s)
        for k in range(len(tiles) - 1)
    ]


def around_even(tiles, s, sub):
    down = [rolled(t, s) for t in tiles]
    if 2 * s == SUB:
        return [a + b for a, b in zip(down[1:], down[:-1])]
    return [
        jnp.where(sub == 0, down[k - 1], down[k]) + rolled(tiles[k], -s)
        for k in range(1, len(tiles))
    ]


def weight(value, chosen):
    return jnp.where(chosen, jnp.float32(value), jnp.float32(0.0))


def lift_rows(tiles, s, sub, has_left, has_right):
    odd = weight(0.5, sub % (2 * s) == s)
    even = weight(0.25, sub % (2 * s) == 0)
    left, right = tiles[0], tiles[-1]
    inner = [t - odd * n for t, n in zip(tiles[1:-1], around_odd(tiles[1:], s, sub))]
    ahead = rolled(tiles[1], -s)
    left = left - jnp.where(sub == SUB - s, 0.5 * has_left * ahead, 0.0)
    smooth = [t + even * n for t, n in zip(inner, around_even([left] + inner, s, sub))]
    behind = rolled(inner[-1], s)
    if s == 1:
        right = jnp.where(sub == 0, rolled(right, -1) + 0.25 * has_right * behind, right)
        left = left + jnp.where(sub == SUB - 2, 0.25 * rolled(left, -1), 0.0)
    elif s == 2:
        right = jnp.where(
            sub == 0, 0.875 * right + rolled(right, -2) + 0.25 * has_right * behind, right
        )
        left = left + jnp.where(sub == SUB - 4, 0.25 * rolled(left, -2), 0.0)
    return [left] + smooth + [right]


def combine(first, second, scale):
    return [a + scale * b for a, b in zip(first, second)]


def front_parts(c):
    d1, d3, d5 = (combine(c[k], combine(c[k - 1], c[k + 1], 1.0), -0.5) for k in (1, 3, 5))
    c2 = combine(c[2], combine(d1, d3, 1.0), 0.25)
    c4 = combine(c[4], combine(d3, d5, 1.0), 0.25)
    third = [0.25 * (a - 0.5 * b) for a, b in zip(c2, c4)]
    return c[0], combine(c[0], d1, 0.25), third


def back_parts(c):
    d = {k: combine(c[k], combine(c[k - 1], c[k + 1], 1.0), -0.5) for k in (3, 5, 7, 9, 11, 13)}
    e = {k: combine(c[k], combine(d[k - 1], d[k + 1], 1.0), 0.25) for k in (4, 6, 8, 10, 12)}
    d6 = combine(e[6], combine(e[4], e[8], 1.0), -0.5)
    d10 = combine(e[10], combine(e[8], e[12], 1.0), -0.5)
    f8 = combine(e[8], combine(d6, d10, 1.0), 0.25)
    first = combine(c[15], c[14], -0.5)
    second = combine(combine(c[14], d[13], 0.25), e[12], -0.5)
    third = combine(combine(e[12], d10, 0.25), f8, -0.5)
    return first, second, third


def count_kept(mask_ref, counts_ref, starts_ref):
    rows = mask_ref.shape[0]
    kept = mask_ref[:, 0, :]
    for t in range(1, mask_ref.shape[1]):
        kept = kept + mask_ref[:, t, :]
    kept = jnp.sum(kept.astype(jnp.float32), axis=1, keepdims=True)
    kept = jnp.broadcast_to(kept, (rows, LANES))
    shape = (rows, rows)
    later = lax.broadcasted_iota(jnp.int32, shape, 0) > lax.broadcasted_iota(jnp.int32, shape, 1)
    later = jnp.where(later, jnp.float32(1.0), jnp.float32(0.0)).astype(jnp.bfloat16)
    starts = jnp.dot(later, kept.astype(jnp.bfloat16), preferred_element_type=jnp.float32)
    starts_ref[...] = starts.astype(jnp.int32)
    total = (starts[rows - 1 :, :] + kept[rows - 1 :, :]).astype(jnp.int32)
    counts_ref[...] = jnp.broadcast_to(total, counts_ref.shape)


def y_edges_kernel(source_ref, inner_ref, outer_ref, snapshot_ref, sems):
    rows, cols, depth = snapshot_ref.shape
    half = rows // 2
    cuts = [(0, SUB), (cols - 2 * SUB, cols), (SUB, cols - 2 * SUB)]
    copies = [
        pltpu.make_async_copy(source_ref.at[:, a:b, :], snapshot_ref.at[:, a:b, :], sems.at[k])
        for k, (a, b) in enumerate(cuts)
    ]
    for copy in copies:
        copy.start()
    even_gy = is_even("gy")
    sub = sublane()
    zero = jnp.zeros((SUB, LANES), jnp.float32)

    def before(x, lanes):
        v = snapshot_ref[x, :SUB, lanes]
        d1 = v - weight(0.5, sub % 2 == 1) * (rolled(v, -1) + rolled(v, 1))
        c2 = d1 + 0.25 * (rolled(d1, -1) + rolled(d1, 1))
        second = rolled(v, 1) + 0.25 * d1
        third = 0.25 * (c2 - 0.5 * rolled(c2, -2))
        return jnp.where(
            sub == 0, v, jnp.where(sub == 1, second, jnp.where(sub == 2, third, 0.0))
        )

    def after(x, lanes):
        last = [snapshot_ref[x, cols - n * SUB : cols - (n - 1) * SUB, lanes] for n in (2, 1)]
        v = [zero] + last + [zero]
        odd = weight(0.5, sub % 2 == 1)
        d = [zero] + [t - odd * n for t, n in zip(v[1:-1], neighbours(v, 1, sub))] + [zero]
        even = weight(0.25, sub % 2 == 0)
        e = [zero] + [t + even * n for t, n in zip(d[1:-1], neighbours(d, 1, sub))] + [zero]
        odd = weight(0.5, sub % 4 == 2)
        f = [zero] + [t - odd * n for t, n in zip(e[1:-1], neighbours(e, 2, sub))] + [zero]
        even = weight(0.25, sub % 4 == 0)
        g = [t + even * n for t, n in zip(f[1:-1], neighbours(f, 2, sub))]
        first = d[2]
        second = v[2] + 0.25 * rolled(d[2], 1) - 0.5 * rolled(e[2], 2)
        third = e[2] + 0.25 * rolled(f[2], 2) - 0.5 * rolled(g[1], 4)
        return jnp.where(
            sub == 7, first, jnp.where(sub == 6, second, jnp.where(sub == 4, third, 0.0))
        )

    for copy in copies[:2]:
        copy.wait()

    @pl.loop(0, half)
    def _(x):
        for t in range(depth // LANES):
            lanes = slice(t * LANES, (t + 1) * LANES)
            to_before = before(x, lanes) + rolled(before(x + half, lanes), 4)
            to_after = after(x, lanes) + rolled(after(x + half, lanes), 4)
            inner_ref[x, :, lanes] = jnp.where(even_gy, to_after, to_before)
            outer_ref[x, :, lanes] = jnp.where(even_gy, to_before, to_after)

    copies[2].wait()


def y_edges(snapshot):
    rows, cols, depth = snapshot.shape
    shape = jax.ShapeDtypeStruct((rows // 2, SUB, depth), jnp.float32)
    return pl.pallas_call(
        y_edges_kernel,
        in_specs=[pl.BlockSpec(memory_space=pltpu.HBM)],
        out_specs=[VMEM] * 3,
        out_shape=[shape, shape, jax.ShapeDtypeStruct(snapshot.shape, jnp.float32)],
        scratch_shapes=[pltpu.SemaphoreType.DMA((3,))],
        compiler_params=pltpu.CompilerParams(vmem_limit_bytes=EDGE_LIMIT),
        name="y_edges",
    )(snapshot)


def x_edges_inner_kernel(
    snapshot_ref, mask_ref, inner_ref, outer_ref, counts_ref, starts_ref
):
    rows, cols, depth = snapshot_ref.shape
    even_gx = is_even("gx")
    count_kept(mask_ref, counts_ref, starts_ref)

    @pl.loop(0, cols // SUB)
    def _(k):
        here = pl.ds(pl.multiple_of(SUB * k, SUB), SUB)
        placed = pl.ds(pl.multiple_of(SUB * k + SUB, SUB), SUB)
        for t in range(depth // LANES):
            lanes = slice(t * LANES, (t + 1) * LANES)
            c = {x: [snapshot_ref[x, here, lanes]] for x in range(rows)}
            for level, (a, b) in enumerate(zip(front_parts(c), back_parts(c))):
                inner_ref[level, placed, lanes] = jnp.where(even_gx, b[0], a[0])
                outer_ref[level, placed, lanes] = jnp.where(even_gx, a[0], b[0])


def x_edges_halo_kernel(y_inner_ref, y_outer_ref, _, __, inner_ref, outer_ref):
    half, _, depth = y_inner_ref.shape
    rows = 2 * half
    cols = inner_ref.shape[1] - 2 * SUB
    sub = sublane()
    gy = lax.axis_index("gy")
    even_gy, even_gx = is_even("gy"), is_even("gx")

    @pl.loop(0, depth // LANES)
    def _(t):
        lanes = pl.ds(pl.multiple_of(t * LANES, LANES), LANES)
        for place in (0, cols + SUB):
            if place == 0:
                held, swap = (sub >= 4) & (gy > 0), even_gy
            else:
                held, swap = (sub < 4) & (gy < lax.axis_size("gy") - 1), ~even_gy
            packed = [
                jnp.where(swap, y_outer_ref[x, :, lanes], y_inner_ref[x, :, lanes])
                for x in range(half)
            ]
            packed = packed + [rolled(tile, 4) for tile in packed]
            c = {x: [jnp.where(held, packed[x], 0.0)] for x in range(rows)}
            for level, (a, b) in enumerate(zip(front_parts(c), back_parts(c))):
                inner_ref[level, place : place + SUB, lanes] = jnp.where(even_gx, b[0], a[0])
                outer_ref[level, place : place + SUB, lanes] = jnp.where(even_gx, a[0], b[0])


def x_edges_inner(snapshot, mask, devices):
    rows, cols, depth = snapshot.shape
    shape = jax.ShapeDtypeStruct((3, cols + 2 * SUB, depth), jnp.float32)
    return pl.pallas_call(
        x_edges_inner_kernel,
        in_specs=[VMEM] * 2,
        out_specs=[VMEM] * 4,
        out_shape=[
            shape,
            shape,
            jax.ShapeDtypeStruct((devices, LANES), jnp.int32),
            jax.ShapeDtypeStruct((rows, LANES), jnp.int32),
        ],
        compiler_params=PARAMS,
        name="x_edges_inner",
    )(snapshot, mask)


def x_edges_halo(y_inner, y_outer, x_inner, x_outer):
    shape = jax.ShapeDtypeStruct(x_inner.shape, jnp.float32)
    return pl.pallas_call(
        x_edges_halo_kernel,
        in_specs=[VMEM] * 4,
        out_specs=[VMEM] * 2,
        out_shape=[shape] * 2,
        input_output_aliases={2: 0, 3: 1},
        compiler_params=PARAMS,
        name="x_edges_halo",
    )(y_inner, y_outer, x_inner, x_outer)


def lift_kernel(
    scales_ref,
    snapshot_ref,
    y_inner_ref,
    y_outer_ref,
    x_inner_ref,
    x_outer_ref,
    coefficients_hbm_ref,
    front_ref,
    back_ref,
    work,
    sems,
):
    rows, cols, depth = snapshot_ref.shape
    width = depth // LANES
    count = cols // SUB
    sub = sublane()
    gx, gy = lax.axis_index("gx"), lax.axis_index("gy")
    one, zero = jnp.float32(1.0), jnp.float32(0.0)
    x_left = jnp.where(gx > 0, one, zero)
    x_right = jnp.where(gx < lax.axis_size("gx") - 1, one, zero)
    y_left = jnp.where(gy > 0, one, zero)
    y_right = jnp.where(gy < lax.axis_size("gy") - 1, one, zero)

    scale = [scales_ref[k] for k in range(4)]
    factor = {8: jnp.where(sub % 8 == 0, scale[3], scale[2])}
    factor[4] = jnp.where(sub % 4 == 0, scale[2], scale[1])
    factor[2] = jnp.where(sub % 2 == 0, scale[1], scale[0])
    factor[8] = jnp.where(sub % 4 == 0, factor[8], factor[2])
    factor[4] = jnp.where(sub % 4 == 0, factor[4], factor[2])
    factor[1] = jnp.where(sub % 2 == 0, scale[0], scale[0])
    factor[8] = jnp.where(sub % 2 == 0, factor[8], scale[0])
    factor[4] = jnp.where(sub % 2 == 0, factor[4], scale[0])

    even_gx, even_gy = is_even("gx"), is_even("gy")
    left_held = (sub >= 4) & (gy > 0)
    right_held = (sub < 4) & (gy < lax.axis_size("gy") - 1)
    half = rows // 2
    past_at, kept_at, after_at, before_at = range(half, half + 4)

    def write(t):
        lanes = pl.ds(pl.multiple_of(t * LANES, LANES), LANES)
        return [
            pltpu.make_async_copy(
                ref.at[:, :, lanes], coefficients_hbm_ref.at[at : at + half, :, lanes], sems.at[t, i]
            )
            for i, (ref, at) in enumerate(((front_ref, 0), (back_ref, half)))
        ]

    @pl.loop(0, width)
    def _(t):
        lanes = pl.ds(pl.multiple_of(t * LANES, LANES), LANES)

        def span(k):
            return slice(SUB * k, SUB * (k + 1))

        def store(x, k, tile):
            if 1 <= k <= count:
                by = 8 if x % 8 == 0 else 4 if x % 4 == 0 else 2 if x % 2 == 0 else 1
                ref = front_ref if x < half else back_ref
                ref[x % half, span(k - 1), lanes] = factor[by] * tile

        def entry(x, k):
            if 1 <= k <= count:
                return snapshot_ref[x, span(k - 1), lanes]
            inner, outer = y_inner_ref[x % half, :, lanes], y_outer_ref[x % half, :, lanes]
            tile = jnp.where(even_gy if k == 0 else ~even_gy, outer, inner)
            tile = rolled(tile, 4) if x >= half else tile
            return jnp.where(left_held if k == 0 else right_held, tile, 0.0)

        def before(level, k):
            inner, outer = x_inner_ref[level, span(k), lanes], x_outer_ref[level, span(k), lanes]
            return jnp.where(even_gx, outer, inner)

        def after(level, k):
            inner, outer = x_inner_ref[level, span(k), lanes], x_outer_ref[level, span(k), lanes]
            return jnp.where(even_gx, inner, outer)

        def step(c, s, beyond, ahead):
            held = sub % s == 0
            half_w, quarter_w = (weight(0.5, held), weight(0.25, held)) if s > 1 else (0.5, 0.25)
            c[rows] = beyond
            for x in range(s, rows, 2 * s):
                c[x] = c[x] - half_w * (c[x - s] + c[x + s])
            c[-s] = ahead - (half_w * x_left) * c[0]
            for x in range(0, rows, 2 * s):
                c[x] = c[x] + quarter_w * (c[x - s] + c[x + s])
            return c

        def lift_row(source, target, s):
            row = [source(k) for k in range(count + 2)]
            for k, tile in enumerate(lift_rows(row, s, sub, y_left, y_right)):
                target(k, tile)

        def held_at(at):
            return lambda k: work[at, span(k)]

        def put_at(at):
            def put(k, tile):
                work[at, span(k)] = tile

            return put

        for k in range(count + 2):
            c = {x: entry(x, k) for x in range(rows)}
            c = step(c, 1, after(0, k), before(0, k))
            for x in range(1, rows, 2):
                store(x, k, c[x])
            for x in range(0, rows, 2):
                work[x // 2, span(k)] = c[x]
            work[past_at, span(k)] = after(1, k) + (0.25 * x_right) * c[rows - 1]
            work[kept_at, span(k)] = before(1, k) + 0.25 * c[-1]
        for at in range(half + 2):
            lift_row(held_at(at), put_at(at), 1)
        lift_row(lambda k: after(2, k), put_at(after_at), 1)
        lift_row(lambda k: before(2, k), put_at(before_at), 1)
        for k in range(count + 2):
            c = {x: work[x // 2, span(k)] for x in range(0, rows, 2)}
            past = work[past_at, span(k)]
            c = step(c, 2, past, work[kept_at, span(k)])
            for x in range(2, rows, 4):
                store(x, k, c[x])
            for x in range(0, rows, 4):
                work[x // 2, span(k)] = c[x]
            mine = 0.875 * past + work[after_at, span(k)]
            work[past_at, span(k)] = mine + (0.25 * x_right) * c[rows - 2]
            work[kept_at, span(k)] = work[before_at, span(k)] + 0.25 * c[-2]
        for at in [x // 2 for x in range(0, rows, 4)] + [past_at, kept_at]:
            lift_row(held_at(at), put_at(at), 2)
        for k in range(count + 2):
            c = {x: work[x // 2, span(k)] for x in range(0, rows, 4)}
            c = step(c, 4, work[past_at, span(k)], work[kept_at, span(k)])
            for x in range(4, rows, 8):
                store(x, k, c[x])
            for x in range(0, rows, 8):
                work[x // 2, span(k)] = c[x]
        for x in range(0, rows, 8):
            lift_row(held_at(x // 2), lambda k, tile, x=x: store(x, k, tile), 4)
        for copy in write(t):
            copy.start()

    @pl.loop(0, width)
    def _(t):
        for copy in write(t):
            copy.wait()


def lift(scales, snapshot, y_inner, y_outer, x_inner, x_outer):
    rows, cols, depth = snapshot.shape
    return pl.pallas_call(
        lift_kernel,
        in_specs=[SMEM] + [VMEM] * 5,
        out_specs=[pl.BlockSpec(memory_space=pltpu.HBM), VMEM],
        out_shape=[
            jax.ShapeDtypeStruct(snapshot.shape, jnp.float32),
            jax.ShapeDtypeStruct((rows // 2, cols, depth), jnp.float32),
        ],
        scratch_shapes=[
            pltpu.VMEM((rows // 2, cols, depth), jnp.float32),
            pltpu.VMEM((rows // 2 + 4, cols + 2 * SUB, LANES), jnp.float32),
            pltpu.SemaphoreType.DMA((depth // LANES, 2)),
        ],
        compiler_params=PARAMS,
        cost_estimate=pl.CostEstimate(
            flops=2 * 10**9, bytes_accessed=16 * 2**20, transcendentals=0
        ),
        name="lift",
    )(scales, snapshot, y_inner, y_outer, x_inner, x_outer)


def pack_kernel(
    table_ref,
    starts_ref,
    coefficients_hbm_ref,
    front_ref,
    flags_ref,
    packed_ref,
    counts_ref,
    back_ref,
    buffer,
    ranks,
    sems,
):
    half, cols, depth = front_ref.shape
    rows = 2 * half
    width = depth // LANES
    slots = rows * cols * width
    per_row = cols * width
    one, zero = jnp.float32(1.0), jnp.float32(0.0)
    parts = sems.shape[0]
    group = half // parts
    copies = [
        pltpu.make_async_copy(
            coefficients_hbm_ref.at[half + group * part : half + group * (part + 1)],
            back_ref.at[group * part : group * (part + 1)],
            sems.at[part],
        )
        for part in range(parts)
    ]
    for copy in copies:
        copy.start()

    device = lax.axis_index("gx") * lax.axis_size("gy") + lax.axis_index("gy")
    table = table_ref[...]
    row_id = lax.broadcasted_iota(jnp.int32, table.shape, 0)
    lane_id = lax.broadcasted_iota(jnp.int32, table.shape, 1)
    offset = jnp.sum(jnp.where(row_id < device, table, 0), axis=0, keepdims=True)[0, 0]
    counts_ref[...] = jnp.sum(jnp.where(row_id == lane_id, table, 0), axis=0, keepdims=True)
    buffer[...] = jnp.zeros_like(buffer)
    flags = flags_ref[...]
    source = lax.broadcasted_iota(jnp.int32, (per_row, per_row), 0)
    target = lax.broadcasted_iota(jnp.int32, (per_row, per_row), 1)
    source = source % cols * width + source // cols
    target = target % cols * width + target // cols
    earlier = jnp.where(source < target, one, zero).astype(jnp.bfloat16)
    place = jnp.dot(flags.astype(jnp.bfloat16), earlier, preferred_element_type=jnp.float32)
    ranks[...] = jnp.where(flags > 0, place.astype(jnp.int32), -per_row)
    span = per_row + SUB

    def place_row(x):
        ref = front_ref if x < half else back_ref
        at = (offset + starts_ref[x, 0]) & (slots - 1)
        base = pl.multiple_of(lax.shift_left(lax.shift_right_logical(at, 3), 3), SUB)
        wanted = ranks[x : x + 1, :] + (at - base)
        row_id = lax.broadcasted_iota(jnp.int32, (span, per_row), 0)
        onehot = jnp.where(row_id == wanted, one, zero).astype(jnp.bfloat16)
        values = jnp.concatenate(
            [ref[x % half, :, LANES * t : LANES * (t + 1)] for t in range(width)], axis=0
        )
        high = values.astype(jnp.bfloat16)
        low = (values - high.astype(jnp.float32)).astype(jnp.bfloat16)
        both = jnp.dot(
            onehot, jnp.concatenate([high, low], axis=1), preferred_element_type=jnp.float32
        )
        buffer[pl.ds(base, span), :] += both[:, :LANES] + both[:, LANES:]

    for x in range(rows):
        if x >= half and x % group == 0:
            copies[(x - half) // group].wait()
        place_row(x)

    packed_ref[span:, :] = buffer[span:slots, :]
    packed_ref[:span, :] = buffer[:span, :] + buffer[slots:, :]


def pack(table, starts, coefficients, front, flags):
    rows, cols, depth = coefficients.shape
    per_row = flags.shape[1]
    slots = rows * per_row
    return pl.pallas_call(
        pack_kernel,
        in_specs=[VMEM, SMEM, pl.BlockSpec(memory_space=pltpu.HBM), VMEM, VMEM],
        out_specs=[VMEM] * 2,
        out_shape=[
            jax.ShapeDtypeStruct((slots, LANES), jnp.float32),
            jax.ShapeDtypeStruct((1, table.shape[0]), jnp.int32),
        ],
        scratch_shapes=[
            pltpu.VMEM((rows // 2, cols, depth), jnp.float32),
            pltpu.VMEM((slots + per_row + SUB, LANES), jnp.float32),
            pltpu.VMEM((rows, per_row), jnp.int32),
            pltpu.SemaphoreType.DMA((2,)),
        ],
        compiler_params=pltpu.CompilerParams(vmem_limit_bytes=PACK_LIMIT),
        name="pack",
    )(table, starts, coefficients, front, flags)


def merge_kernel(counts_ref, arrived_ref, merged_ref):
    devices, share, _ = arrived_ref.shape
    slots = devices * share
    shift = slots.bit_length() - 1
    device = lax.axis_index("gx") * lax.axis_size("gy") + lax.axis_index("gy")
    merged_ref[...] = jnp.zeros_like(merged_ref)
    row_id = lax.broadcasted_iota(jnp.int32, (share, LANES), 0) + device * share

    def one(s, carry):
        start, held = carry
        end = start + counts_ref[0, s]
        block = lax.shift_right_logical(start, shift)
        rows = arrived_ref[s]
        here = row_id >= (start & (slots - 1))
        held = held + jnp.where(here, rows, 0.0)
        following = jnp.where(here, 0.0, rows)
        merged_ref[jnp.minimum(block + 1, devices - 1)] = following
        merged_ref[block] = held
        crossed = lax.shift_right_logical(end, shift) > block
        return end, jnp.where(crossed, following, held)

    empty = jnp.zeros((share, LANES), jnp.float32)
    lax.fori_loop(0, devices, one, (jnp.int32(0), empty), unroll=4)


def merge(counts, arrived):
    return pl.pallas_call(
        merge_kernel,
        in_specs=[SMEM, VMEM],
        out_specs=VMEM,
        out_shape=jax.ShapeDtypeStruct(arrived.shape, jnp.float32),
        compiler_params=PARAMS,
        name="merge",
    )(counts, arrived)


def on_device(snapshot, keep_mask, exponents):
    rows, cols, depth = snapshot.shape
    width = keep_mask.shape[2]
    devices = lax.axis_size("gx") * lax.axis_size("gy")
    slots = rows * cols * width
    mask = keep_mask.transpose(0, 2, 1)
    y_inner, y_outer, held = y_edges(snapshot)
    y_halo = pairs_exchange(y_inner, y_outer, "gy", ring=True)
    x_inner, x_outer, own_counts, starts = x_edges_inner(held, mask, devices)
    table = lax.all_to_all(own_counts.reshape(devices, 1, LANES), ALL, 0, 0, tiled=True)
    table = table.reshape(devices, LANES)
    flags = mask.reshape(rows, cols * width)
    scales = jnp.exp2(exponents.astype(jnp.float32))
    x_halo = pairs_exchange(*x_edges_halo(*y_halo, x_inner, x_outer), "gx", ring=False)
    coefficients, front = lift(scales, snapshot, *y_halo, *x_halo)
    packed, counts = pack(table, starts, coefficients, front, flags)
    share = slots // devices
    arrived = lax.all_to_all(packed.reshape(devices, share, LANES), ALL, 0, 0, tiled=True)
    merged = merge(counts, arrived)
    stream = lax.all_to_all(merged, ALL, 0, 0, tiled=True).reshape(slots, LANES)
    return coefficients, stream


def solution(mesh):
    in_specs = (P("gx", "gy", None), P("gx", "gy", None), P())
    out_specs = (P("gx", "gy", None), P(("gx", "gy"), None))
    return jax.shard_map(
        on_device, mesh=mesh, in_specs=in_specs, out_specs=out_specs, check_vma=False
    )
```

```python
import jax
import jax.numpy as jnp
from jax import lax
from jax.experimental import pallas as pl
from jax.experimental.pallas import tpu as pltpu
from jax.sharding import PartitionSpec as P

ALL = ("gx", "gy")
SUB = 8
LANES = 128
EDGE_LIMIT = 50 * 2**20
PACK_LIMIT = 50 * 2**20
VMEM = pl.BlockSpec(memory_space=pltpu.VMEM)
SMEM = pl.BlockSpec(memory_space=pltpu.SMEM)
PARAMS = pltpu.CompilerParams(vmem_limit_bytes=16 * 2**20)


def pairs_exchange(first, second, axis, ring):
    count = lax.axis_size(axis)
    inner = [(k, k ^ 1) for k in range(count)]
    outer = [(k, k + 1 if k % 2 else k - 1) for k in range(0 if ring else 1, count - (not ring))]
    outer = [(a % count, b % count) for a, b in outer]
    return lax.ppermute(first, axis, inner), lax.ppermute(second, axis, outer)


def is_even(axis):
    return lax.axis_index(axis) % 2 == 0


def sublane():
    return lax.broadcasted_iota(jnp.int32, (SUB, LANES), 0)


def rolled(tile, steps):
    return pltpu.roll(tile, steps % SUB, 0)


def neighbours(tiles, s, sub):
    up = [rolled(t, -s) for t in tiles]
    down = up if 2 * s == SUB else [rolled(t, s) for t in tiles]
    return [
        jnp.where(sub < SUB - s, up[k], up[k + 1]) + jnp.where(sub >= s, down[k], down[k - 1])
        for k in range(1, len(tiles) - 1)
    ]


def around_odd(tiles, s, sub):
    up = [rolled(t, -s) for t in tiles]
    if 2 * s == SUB:
        return [a + b for a, b in zip(up[:-1], up[1:])]
    return [
        jnp.where(sub == SUB - s, up[k + 1], up[k]) + rolled(tiles[k], s)
        for k in range(len(tiles) - 1)
    ]


def around_even(tiles, s, sub):
    down = [rolled(t, s) for t in tiles]
    if 2 * s == SUB:
        return [a + b for a, b in zip(down[1:], down[:-1])]
    return [
        jnp.where(sub == 0, down[k - 1], down[k]) + rolled(tiles[k], -s)
        for k in range(1, len(tiles))
    ]


def weight(value, chosen):
    return jnp.where(chosen, jnp.float32(value), jnp.float32(0.0))


def lift_rows(tiles, s, sub, has_left, has_right):
    odd = weight(0.5, sub % (2 * s) == s)
    even = weight(0.25, sub % (2 * s) == 0)
    left, right = tiles[0], tiles[-1]
    inner = [t - odd * n for t, n in zip(tiles[1:-1], around_odd(tiles[1:], s, sub))]
    ahead = rolled(tiles[1], -s)
    left = left - jnp.where(sub == SUB - s, 0.5 * has_left * ahead, 0.0)
    smooth = [t + even * n for t, n in zip(inner, around_even([left] + inner, s, sub))]
    behind = rolled(inner[-1], s)
    if s == 1:
        right = jnp.where(sub == 0, rolled(right, -1) + 0.25 * has_right * behind, right)
        left = left + jnp.where(sub == SUB - 2, 0.25 * rolled(left, -1), 0.0)
    elif s == 2:
        right = jnp.where(
            sub == 0, 0.875 * right + rolled(right, -2) + 0.25 * has_right * behind, right
        )
        left = left + jnp.where(sub == SUB - 4, 0.25 * rolled(left, -2), 0.0)
    return [left] + smooth + [right]


def combine(first, second, scale):
    return [a + scale * b for a, b in zip(first, second)]


def front_parts(c):
    d1, d3, d5 = (combine(c[k], combine(c[k - 1], c[k + 1], 1.0), -0.5) for k in (1, 3, 5))
    c2 = combine(c[2], combine(d1, d3, 1.0), 0.25)
    c4 = combine(c[4], combine(d3, d5, 1.0), 0.25)
    third = [0.25 * (a - 0.5 * b) for a, b in zip(c2, c4)]
    return c[0], combine(c[0], d1, 0.25), third


def back_parts(c):
    d = {k: combine(c[k], combine(c[k - 1], c[k + 1], 1.0), -0.5) for k in (3, 5, 7, 9, 11, 13)}
    e = {k: combine(c[k], combine(d[k - 1], d[k + 1], 1.0), 0.25) for k in (4, 6, 8, 10, 12)}
    d6 = combine(e[6], combine(e[4], e[8], 1.0), -0.5)
    d10 = combine(e[10], combine(e[8], e[12], 1.0), -0.5)
    f8 = combine(e[8], combine(d6, d10, 1.0), 0.25)
    first = combine(c[15], c[14], -0.5)
    second = combine(combine(c[14], d[13], 0.25), e[12], -0.5)
    third = combine(combine(e[12], d10, 0.25), f8, -0.5)
    return first, second, third


def count_kept(mask_ref, counts_ref, starts_ref):
    rows = mask_ref.shape[0]
    kept = mask_ref[:, 0, :]
    for t in range(1, mask_ref.shape[1]):
        kept = kept + mask_ref[:, t, :]
    kept = jnp.sum(kept.astype(jnp.float32), axis=1, keepdims=True)
    kept = jnp.broadcast_to(kept, (rows, LANES))
    shape = (rows, rows)
    later = lax.broadcasted_iota(jnp.int32, shape, 0) > lax.broadcasted_iota(jnp.int32, shape, 1)
    later = jnp.where(later, jnp.float32(1.0), jnp.float32(0.0)).astype(jnp.bfloat16)
    starts = jnp.dot(later, kept.astype(jnp.bfloat16), preferred_element_type=jnp.float32)
    starts_ref[...] = starts.astype(jnp.int32)
    total = (starts[rows - 1 :, :] + kept[rows - 1 :, :]).astype(jnp.int32)
    counts_ref[...] = jnp.broadcast_to(total, counts_ref.shape)


def y_edges_kernel(source_ref, inner_ref, outer_ref, snapshot_ref, sems):
    rows, cols, depth = snapshot_ref.shape
    half = rows // 2
    cuts = [(0, SUB), (cols - 2 * SUB, cols), (SUB, cols - 2 * SUB)]
    copies = [
        pltpu.make_async_copy(source_ref.at[:, a:b, :], snapshot_ref.at[:, a:b, :], sems.at[k])
        for k, (a, b) in enumerate(cuts)
    ]
    for copy in copies:
        copy.start()
    even_gy = is_even("gy")
    sub = sublane()
    zero = jnp.zeros((SUB, LANES), jnp.float32)

    def before(x, lanes):
        v = snapshot_ref[x, :SUB, lanes]
        d1 = v - weight(0.5, sub % 2 == 1) * (rolled(v, -1) + rolled(v, 1))
        c2 = d1 + 0.25 * (rolled(d1, -1) + rolled(d1, 1))
        second = rolled(v, 1) + 0.25 * d1
        third = 0.25 * (c2 - 0.5 * rolled(c2, -2))
        return jnp.where(
            sub == 0, v, jnp.where(sub == 1, second, jnp.where(sub == 2, third, 0.0))
        )

    def after(x, lanes):
        last = [snapshot_ref[x, cols - n * SUB : cols - (n - 1) * SUB, lanes] for n in (2, 1)]
        v = [zero] + last + [zero]
        odd = weight(0.5, sub % 2 == 1)
        d = [zero] + [t - odd * n for t, n in zip(v[1:-1], neighbours(v, 1, sub))] + [zero]
        even = weight(0.25, sub % 2 == 0)
        e = [zero] + [t + even * n for t, n in zip(d[1:-1], neighbours(d, 1, sub))] + [zero]
        odd = weight(0.5, sub % 4 == 2)
        f = [zero] + [t - odd * n for t, n in zip(e[1:-1], neighbours(e, 2, sub))] + [zero]
        even = weight(0.25, sub % 4 == 0)
        g = [t + even * n for t, n in zip(f[1:-1], neighbours(f, 2, sub))]
        first = d[2]
        second = v[2] + 0.25 * rolled(d[2], 1) - 0.5 * rolled(e[2], 2)
        third = e[2] + 0.25 * rolled(f[2], 2) - 0.5 * rolled(g[1], 4)
        return jnp.where(
            sub == 7, first, jnp.where(sub == 6, second, jnp.where(sub == 4, third, 0.0))
        )

    for copy in copies[:2]:
        copy.wait()

    @pl.loop(0, half)
    def _(x):
        for t in range(depth // LANES):
            lanes = slice(t * LANES, (t + 1) * LANES)
            to_before = before(x, lanes) + rolled(before(x + half, lanes), 4)
            to_after = after(x, lanes) + rolled(after(x + half, lanes), 4)
            inner_ref[x, :, lanes] = jnp.where(even_gy, to_after, to_before)
            outer_ref[x, :, lanes] = jnp.where(even_gy, to_before, to_after)

    copies[2].wait()


def y_edges(snapshot):
    rows, cols, depth = snapshot.shape
    shape = jax.ShapeDtypeStruct((rows // 2, SUB, depth), jnp.float32)
    return pl.pallas_call(
        y_edges_kernel,
        in_specs=[pl.BlockSpec(memory_space=pltpu.HBM)],
        out_specs=[VMEM] * 3,
        out_shape=[shape, shape, jax.ShapeDtypeStruct(snapshot.shape, jnp.float32)],
        scratch_shapes=[pltpu.SemaphoreType.DMA((3,))],
        compiler_params=pltpu.CompilerParams(vmem_limit_bytes=EDGE_LIMIT),
        name="y_edges",
    )(snapshot)


def x_edges_inner_kernel(
    snapshot_ref, mask_ref, inner_ref, outer_ref, counts_ref, starts_ref
):
    rows, cols, depth = snapshot_ref.shape
    even_gx = is_even("gx")
    count_kept(mask_ref, counts_ref, starts_ref)

    @pl.loop(0, cols // SUB)
    def _(k):
        here = pl.ds(pl.multiple_of(SUB * k, SUB), SUB)
        placed = pl.ds(pl.multiple_of(SUB * k + SUB, SUB), SUB)
        for t in range(depth // LANES):
            lanes = slice(t * LANES, (t + 1) * LANES)
            c = {x: [snapshot_ref[x, here, lanes]] for x in range(rows)}
            for level, (a, b) in enumerate(zip(front_parts(c), back_parts(c))):
                inner_ref[level, placed, lanes] = jnp.where(even_gx, b[0], a[0])
                outer_ref[level, placed, lanes] = jnp.where(even_gx, a[0], b[0])


def x_edges_halo_kernel(y_inner_ref, y_outer_ref, _, __, inner_ref, outer_ref):
    half, _, depth = y_inner_ref.shape
    rows = 2 * half
    cols = inner_ref.shape[1] - 2 * SUB
    sub = sublane()
    gy = lax.axis_index("gy")
    even_gy, even_gx = is_even("gy"), is_even("gx")

    @pl.loop(0, depth // LANES)
    def _(t):
        lanes = pl.ds(pl.multiple_of(t * LANES, LANES), LANES)
        for place in (0, cols + SUB):
            if place == 0:
                held, swap = (sub >= 4) & (gy > 0), even_gy
            else:
                held, swap = (sub < 4) & (gy < lax.axis_size("gy") - 1), ~even_gy
            packed = [
                jnp.where(swap, y_outer_ref[x, :, lanes], y_inner_ref[x, :, lanes])
                for x in range(half)
            ]
            packed = packed + [rolled(tile, 4) for tile in packed]
            c = {x: [jnp.where(held, packed[x], 0.0)] for x in range(rows)}
            for level, (a, b) in enumerate(zip(front_parts(c), back_parts(c))):
                inner_ref[level, place : place + SUB, lanes] = jnp.where(even_gx, b[0], a[0])
                outer_ref[level, place : place + SUB, lanes] = jnp.where(even_gx, a[0], b[0])


def x_edges_inner(snapshot, mask, devices):
    rows, cols, depth = snapshot.shape
    shape = jax.ShapeDtypeStruct((3, cols + 2 * SUB, depth), jnp.float32)
    return pl.pallas_call(
        x_edges_inner_kernel,
        in_specs=[VMEM] * 2,
        out_specs=[VMEM] * 4,
        out_shape=[
            shape,
            shape,
            jax.ShapeDtypeStruct((devices, LANES), jnp.int32),
            jax.ShapeDtypeStruct((rows, LANES), jnp.int32),
        ],
        compiler_params=PARAMS,
        name="x_edges_inner",
    )(snapshot, mask)


def x_edges_halo(y_inner, y_outer, x_inner, x_outer):
    shape = jax.ShapeDtypeStruct(x_inner.shape, jnp.float32)
    return pl.pallas_call(
        x_edges_halo_kernel,
        in_specs=[VMEM] * 4,
        out_specs=[VMEM] * 2,
        out_shape=[shape] * 2,
        input_output_aliases={2: 0, 3: 1},
        compiler_params=PARAMS,
        name="x_edges_halo",
    )(y_inner, y_outer, x_inner, x_outer)


def lift_kernel(
    scales_ref,
    snapshot_ref,
    y_inner_ref,
    y_outer_ref,
    x_inner_ref,
    x_outer_ref,
    coefficients_hbm_ref,
    front_ref,
    back_ref,
    work,
    sems,
):
    rows, cols, depth = snapshot_ref.shape
    width = depth // LANES
    count = cols // SUB
    sub = sublane()
    gx, gy = lax.axis_index("gx"), lax.axis_index("gy")
    one, zero = jnp.float32(1.0), jnp.float32(0.0)
    x_left = jnp.where(gx > 0, one, zero)
    x_right = jnp.where(gx < lax.axis_size("gx") - 1, one, zero)
    y_left = jnp.where(gy > 0, one, zero)
    y_right = jnp.where(gy < lax.axis_size("gy") - 1, one, zero)

    scale = [scales_ref[k] for k in range(4)]
    factor = {8: jnp.where(sub % 8 == 0, scale[3], scale[2])}
    factor[4] = jnp.where(sub % 4 == 0, scale[2], scale[1])
    factor[2] = jnp.where(sub % 2 == 0, scale[1], scale[0])
    factor[8] = jnp.where(sub % 4 == 0, factor[8], factor[2])
    factor[4] = jnp.where(sub % 4 == 0, factor[4], factor[2])
    factor[1] = jnp.where(sub % 2 == 0, scale[0], scale[0])
    factor[8] = jnp.where(sub % 2 == 0, factor[8], scale[0])
    factor[4] = jnp.where(sub % 2 == 0, factor[4], scale[0])

    even_gx, even_gy = is_even("gx"), is_even("gy")
    left_held = (sub >= 4) & (gy > 0)
    right_held = (sub < 4) & (gy < lax.axis_size("gy") - 1)
    half = rows // 2
    past_at, kept_at, after_at, before_at = range(half, half + 4)

    def write(t):
        lanes = pl.ds(pl.multiple_of(t * LANES, LANES), LANES)
        return [
            pltpu.make_async_copy(
                ref.at[:, :, lanes], coefficients_hbm_ref.at[at : at + half, :, lanes], sems.at[t, i]
            )
            for i, (ref, at) in enumerate(((front_ref, 0), (back_ref, half)))
        ]

    @pl.loop(0, width)
    def _(t):
        lanes = pl.ds(pl.multiple_of(t * LANES, LANES), LANES)

        def span(k):
            return slice(SUB * k, SUB * (k + 1))

        def store(x, k, tile):
            if 1 <= k <= count:
                by = 8 if x % 8 == 0 else 4 if x % 4 == 0 else 2 if x % 2 == 0 else 1
                ref = front_ref if x < half else back_ref
                ref[x % half, span(k - 1), lanes] = factor[by] * tile

        def entry(x, k):
            if 1 <= k <= count:
                return snapshot_ref[x, span(k - 1), lanes]
            inner, outer = y_inner_ref[x % half, :, lanes], y_outer_ref[x % half, :, lanes]
            tile = jnp.where(even_gy if k == 0 else ~even_gy, outer, inner)
            tile = rolled(tile, 4) if x >= half else tile
            return jnp.where(left_held if k == 0 else right_held, tile, 0.0)

        def before(level, k):
            inner, outer = x_inner_ref[level, span(k), lanes], x_outer_ref[level, span(k), lanes]
            return jnp.where(gx > 0, jnp.where(even_gx, outer, inner), 0.0)

        def after(level, k):
            inner, outer = x_inner_ref[level, span(k), lanes], x_outer_ref[level, span(k), lanes]
            return jnp.where(gx < lax.axis_size("gx") - 1, jnp.where(even_gx, inner, outer), 0.0)

        def step(c, s, beyond, ahead):
            held = sub % s == 0
            half_w, quarter_w = (weight(0.5, held), weight(0.25, held)) if s > 1 else (0.5, 0.25)
            c[rows] = beyond
            for x in range(s, rows, 2 * s):
                c[x] = c[x] - half_w * (c[x - s] + c[x + s])
            c[-s] = ahead - (half_w * x_left) * c[0]
            for x in range(0, rows, 2 * s):
                c[x] = c[x] + quarter_w * (c[x - s] + c[x + s])
            return c

        def lift_row(source, target, s):
            row = [source(k) for k in range(count + 2)]
            for k, tile in enumerate(lift_rows(row, s, sub, y_left, y_right)):
                target(k, tile)

        def held_at(at):
            return lambda k: work[at, span(k)]

        def put_at(at):
            def put(k, tile):
                work[at, span(k)] = tile

            return put

        for k in range(count + 2):
            c = {x: entry(x, k) for x in range(rows)}
            c = step(c, 1, after(0, k), before(0, k))
            for x in range(1, rows, 2):
                store(x, k, c[x])
            for x in range(0, rows, 2):
                work[x // 2, span(k)] = c[x]
            work[past_at, span(k)] = after(1, k) + (0.25 * x_right) * c[rows - 1]
            work[kept_at, span(k)] = before(1, k) + 0.25 * c[-1]
        for at in range(half + 2):
            lift_row(held_at(at), put_at(at), 1)
        lift_row(lambda k: after(2, k), put_at(after_at), 1)
        lift_row(lambda k: before(2, k), put_at(before_at), 1)
        for k in range(count + 2):
            c = {x: work[x // 2, span(k)] for x in range(0, rows, 2)}
            past = work[past_at, span(k)]
            c = step(c, 2, past, work[kept_at, span(k)])
            for x in range(2, rows, 4):
                store(x, k, c[x])
            for x in range(0, rows, 4):
                work[x // 2, span(k)] = c[x]
            mine = 0.875 * past + work[after_at, span(k)]
            work[past_at, span(k)] = mine + (0.25 * x_right) * c[rows - 2]
            work[kept_at, span(k)] = work[before_at, span(k)] + 0.25 * c[-2]
        for at in [x // 2 for x in range(0, rows, 4)] + [past_at, kept_at]:
            lift_row(held_at(at), put_at(at), 2)
        for k in range(count + 2):
            c = {x: work[x // 2, span(k)] for x in range(0, rows, 4)}
            c = step(c, 4, work[past_at, span(k)], work[kept_at, span(k)])
            for x in range(4, rows, 8):
                store(x, k, c[x])
            for x in range(0, rows, 8):
                work[x // 2, span(k)] = c[x]
        for x in range(0, rows, 8):
            lift_row(held_at(x // 2), lambda k, tile, x=x: store(x, k, tile), 4)
        for copy in write(t):
            copy.start()

    @pl.loop(0, width)
    def _(t):
        for copy in write(t):
            copy.wait()


def lift(scales, snapshot, y_inner, y_outer, x_inner, x_outer):
    rows, cols, depth = snapshot.shape
    return pl.pallas_call(
        lift_kernel,
        in_specs=[SMEM] + [VMEM] * 5,
        out_specs=[pl.BlockSpec(memory_space=pltpu.HBM), VMEM],
        out_shape=[
            jax.ShapeDtypeStruct(snapshot.shape, jnp.float32),
            jax.ShapeDtypeStruct((rows // 2, cols, depth), jnp.float32),
        ],
        scratch_shapes=[
            pltpu.VMEM((rows // 2, cols, depth), jnp.float32),
            pltpu.VMEM((rows // 2 + 4, cols + 2 * SUB, LANES), jnp.float32),
            pltpu.SemaphoreType.DMA((depth // LANES, 2)),
        ],
        compiler_params=PARAMS,
        cost_estimate=pl.CostEstimate(
            flops=2 * 10**9, bytes_accessed=16 * 2**20, transcendentals=0
        ),
        name="lift",
    )(scales, snapshot, y_inner, y_outer, x_inner, x_outer)


def pack_kernel(
    table_ref,
    starts_ref,
    coefficients_hbm_ref,
    front_ref,
    flags_ref,
    packed_ref,
    counts_ref,
    back_ref,
    buffer,
    ranks,
    sems,
):
    half, cols, depth = front_ref.shape
    rows = 2 * half
    width = depth // LANES
    slots = rows * cols * width
    per_row = cols * width
    one, zero = jnp.float32(1.0), jnp.float32(0.0)
    parts = sems.shape[0]
    group = half // parts
    copies = [
        pltpu.make_async_copy(
            coefficients_hbm_ref.at[half + group * part : half + group * (part + 1)],
            back_ref.at[group * part : group * (part + 1)],
            sems.at[part],
        )
        for part in range(parts)
    ]
    for copy in copies:
        copy.start()

    device = lax.axis_index("gx") * lax.axis_size("gy") + lax.axis_index("gy")
    table = table_ref[...]
    row_id = lax.broadcasted_iota(jnp.int32, table.shape, 0)
    lane_id = lax.broadcasted_iota(jnp.int32, table.shape, 1)
    offset = jnp.sum(jnp.where(row_id < device, table, 0), axis=0, keepdims=True)[0, 0]
    counts_ref[...] = jnp.sum(jnp.where(row_id == lane_id, table, 0), axis=0, keepdims=True)
    buffer[...] = jnp.zeros_like(buffer)
    flags = flags_ref[...]
    source = lax.broadcasted_iota(jnp.int32, (per_row, per_row), 0)
    target = lax.broadcasted_iota(jnp.int32, (per_row, per_row), 1)
    source = source % cols * width + source // cols
    target = target % cols * width + target // cols
    earlier = jnp.where(source < target, one, zero).astype(jnp.bfloat16)
    place = jnp.dot(flags.astype(jnp.bfloat16), earlier, preferred_element_type=jnp.float32)
    ranks[...] = jnp.where(flags > 0, place.astype(jnp.int32), -per_row)
    span = per_row + SUB

    def place_row(x):
        ref = front_ref if x < half else back_ref
        at = (offset + starts_ref[x, 0]) & (slots - 1)
        base = pl.multiple_of(lax.shift_left(lax.shift_right_logical(at, 3), 3), SUB)
        wanted = ranks[x : x + 1, :] + (at - base)
        row_id = lax.broadcasted_iota(jnp.int32, (span, per_row), 0)
        onehot = jnp.where(row_id == wanted, one, zero).astype(jnp.bfloat16)
        values = jnp.concatenate(
            [ref[x % half, :, LANES * t : LANES * (t + 1)] for t in range(width)], axis=0
        )
        high = values.astype(jnp.bfloat16)
        low = (values - high.astype(jnp.float32)).astype(jnp.bfloat16)
        both = jnp.dot(
            onehot, jnp.concatenate([high, low], axis=1), preferred_element_type=jnp.float32
        )
        buffer[pl.ds(base, span), :] += both[:, :LANES] + both[:, LANES:]

    for x in range(rows):
        if x >= half and x % group == 0:
            copies[(x - half) // group].wait()
        place_row(x)

    packed_ref[span:, :] = buffer[span:slots, :]
    packed_ref[:span, :] = buffer[:span, :] + buffer[slots:, :]


def pack(table, starts, coefficients, front, flags):
    rows, cols, depth = coefficients.shape
    per_row = flags.shape[1]
    slots = rows * per_row
    return pl.pallas_call(
        pack_kernel,
        in_specs=[VMEM, SMEM, pl.BlockSpec(memory_space=pltpu.HBM), VMEM, VMEM],
        out_specs=[VMEM] * 2,
        out_shape=[
            jax.ShapeDtypeStruct((slots, LANES), jnp.float32),
            jax.ShapeDtypeStruct((1, table.shape[0]), jnp.int32),
        ],
        scratch_shapes=[
            pltpu.VMEM((rows // 2, cols, depth), jnp.float32),
            pltpu.VMEM((slots + per_row + SUB, LANES), jnp.float32),
            pltpu.VMEM((rows, per_row), jnp.int32),
            pltpu.SemaphoreType.DMA((2,)),
        ],
        compiler_params=pltpu.CompilerParams(vmem_limit_bytes=PACK_LIMIT),
        name="pack",
    )(table, starts, coefficients, front, flags)


def merge_kernel(counts_ref, arrived_ref, merged_ref):
    devices, share, _ = arrived_ref.shape
    slots = devices * share
    shift = slots.bit_length() - 1
    device = lax.axis_index("gx") * lax.axis_size("gy") + lax.axis_index("gy")
    merged_ref[...] = jnp.zeros_like(merged_ref)
    row_id = lax.broadcasted_iota(jnp.int32, (share, LANES), 0) + device * share

    def one(s, carry):
        start, held = carry
        end = start + counts_ref[0, s]
        block = lax.shift_right_logical(start, shift)
        rows = arrived_ref[s]
        here = row_id >= (start & (slots - 1))
        held = held + jnp.where(here, rows, 0.0)
        following = jnp.where(here, 0.0, rows)
        merged_ref[jnp.minimum(block + 1, devices - 1)] = following
        merged_ref[block] = held
        crossed = lax.shift_right_logical(end, shift) > block
        return end, jnp.where(crossed, following, held)

    empty = jnp.zeros((share, LANES), jnp.float32)
    lax.fori_loop(0, devices, one, (jnp.int32(0), empty), unroll=4)


def merge(counts, arrived):
    return pl.pallas_call(
        merge_kernel,
        in_specs=[SMEM, VMEM],
        out_specs=VMEM,
        out_shape=jax.ShapeDtypeStruct(arrived.shape, jnp.float32),
        compiler_params=PARAMS,
        name="merge",
    )(counts, arrived)


def on_device(snapshot, keep_mask, exponents):
    rows, cols, depth = snapshot.shape
    width = keep_mask.shape[2]
    devices = lax.axis_size("gx") * lax.axis_size("gy")
    slots = rows * cols * width
    mask = keep_mask.transpose(0, 2, 1)
    y_inner, y_outer, held = y_edges(snapshot)
    y_halo = pairs_exchange(y_inner, y_outer, "gy", ring=True)
    x_inner, x_outer, own_counts, starts = x_edges_inner(held, mask, devices)
    table = lax.all_to_all(own_counts.reshape(devices, 1, LANES), ALL, 0, 0, tiled=True)
    table = table.reshape(devices, LANES)
    flags = mask.reshape(rows, cols * width)
    scales = jnp.exp2(exponents.astype(jnp.float32))
    x_halo = pairs_exchange(*x_edges_halo(*y_halo, x_inner, x_outer), "gx", ring=True)
    coefficients, front = lift(scales, snapshot, *y_halo, *x_halo)
    packed, counts = pack(table, starts, coefficients, front, flags)
    share = slots // devices
    arrived = lax.all_to_all(packed.reshape(devices, share, LANES), ALL, 0, 0, tiled=True)
    merged = merge(counts, arrived)
    stream = lax.all_to_all(merged, ALL, 0, 0, tiled=True).reshape(slots, LANES)
    return coefficients, stream


def solution(mesh):
    in_specs = (P("gx", "gy", None), P("gx", "gy", None), P())
    out_specs = (P("gx", "gy", None), P(("gx", "gy"), None))
    return jax.shard_map(
        on_device, mesh=mesh, in_specs=in_specs, out_specs=out_specs, check_vma=False
    )
```
